256 devices in a mesh: expert: 64 (over x, z, core), tensor: 4 (over y).
Axes of the slice: x: 4, y: 4, z: 8, core: 2. Of those that a mesh axis runs over, the one named last changes fastest.
Arguments:
- member_weights: bfloat16 [128, 3072, 2560], P('expert', 'tensor'), may hold values from -0.109375 to 0.109375
- cluster_ids: int32 [128], replicated, may hold values from 0 to 63, as said below
- merge_counts: int32 [128], replicated, may hold values from 1 to 8
- tokens: bfloat16 [4096, 3072], P('expert'), may hold values from -6 to 6
- routes: int32 [4096, 8], P('expert'), may hold values from 0 to 63, all different within a row; in each aligned block of 64 rows (0 to 63, 64 to 127, ...) at most 16 rows name the same one
Outputs:
- merged_gate_up: bfloat16 [64, 3072, 2560], P('expert', None, 'tensor')
- hidden: bfloat16 [4096, 8, 1280], P('expert', None, 'tensor')
The draws below stay inside these ranges and needn't reach their ends.
Inputs may be any that keep to these rules, and one draw needn't show every extreme that they name: `cluster_ids`: every one of the 64 merged experts has 1 to 4 members, and some merged expert has exactly 4. `routes`: within the 64 rows of one index of expert no merged expert is named more than 16 times, and one is named exactly 16 times.
All inputs are finite; a program needn't handle non-finite values.
Results may differ from the reference program's by a relative error of at most 0.0031.
Values may be sent and summed in bfloat16 or wider, within the bound.
A program may use at most 128 MiB of HBM per device.

```python
import math
import jax
import jax.numpy as jnp
import numpy as np
from jax import lax

D = 3072
FW = 1280
TOP = 8
TOK_DEV = 64
MEMBERS = 128
CLUSTERS = 64
TOKENS = 4096
CAP = 16
N_EXPERT = 64
N_TENSOR = 4


def draw_cluster_ids(key, part):
    key = jax.random.fold_in(key, 11)
    first_key, second_key = jax.random.split(key)
    placing = jax.random.permutation(first_key, MEMBERS)
    shuffled = jax.random.permutation(second_key, CLUSTERS)
    position = jnp.arange(MEMBERS, dtype=jnp.int32)
    beyond = position - CLUSTERS
    paired = shuffled[jnp.clip(1 + (beyond - 3) // 2, 1, CLUSTERS - 1)]
    extra_cluster = jnp.where(beyond < 3, shuffled[0], paired)
    assigned = jnp.where(position < CLUSTERS, position, extra_cluster).astype(jnp.int32)
    return jnp.zeros((MEMBERS,), jnp.int32).at[placing].set(assigned)


def plant(values, stream_key, low, largest):
    longest = values.shape.index(max(values.shape))
    spots = []
    for shift in (0, 1):
        where = [jax.random.randint(jax.random.fold_in(stream_key, axis), (), 0, length) for axis, length in enumerate(values.shape)]
        where[longest] = (where[longest] + shift) % values.shape[longest]
        spots.append(tuple(where))
    return values.at[spots[0]].set(low).at[spots[1]].set(largest)


def steps_of(own_key, dims, cuts, low, high):
    factor_of = 1.0
    for dim, parts in cuts:
        steps = jax.random.uniform(jax.random.fold_in(jax.random.fold_in(own_key, 6), dim), (parts,), jnp.float32, low / len(cuts), high / len(cuts))
        factor_of = factor_of * jnp.repeat(jnp.exp(steps), dims[dim] // parts).reshape((-1,) + (1,) * (len(dims) - 1 - dim))
    return factor_of


def assign_block(stream_key, own, number, rows, count, top, limit, lean):
    sequence = jax.random.permutation(stream_key, count)
    crowded, usual = portions_of(count, rows * top, limit, lean, True), portions_of(count, rows * top, limit, lean, False)
    places = jnp.arange(count)

    def named(lengths, offset_by):
        used = int((lengths > 0).sum())
        fixed = max(1, used // 4)
        moved = fixed + (places - fixed + offset_by * (used - fixed)) % max(1, count - fixed)
        return jnp.zeros((count,), jnp.int32).at[sequence[jnp.where(places < fixed, places, moved)]].set(jnp.asarray(lengths, jnp.int32))

    lengths = jnp.where(number % 4 == 0, named(crowded, number // 4), named(usual, number - number // 4 - 1))
    mixed = jax.random.permutation(jax.random.fold_in(own, 3), count)
    source_of, taker = mixed[0:count // 2 * 2:2], mixed[1:count // 2 * 2:2]
    room = jnp.minimum(lengths[source_of] - 1, limit - lengths[taker]) // 2
    room = jnp.where((source_of == sequence[0]) | (taker == sequence[0]) | (lengths[taker] == 0), 0, jnp.maximum(room, 0))
    moved = jax.random.randint(jax.random.fold_in(own, 4), (count // 2,), 0, 1 << 20) % (room + 1)
    lengths = lengths.at[source_of].add(-moved).at[taker].add(moved)
    labels = jnp.searchsorted(jnp.cumsum(lengths), jnp.arange(rows * top), side="right").astype(jnp.int32)
    listing = labels.reshape(top, rows).T
    listing = listing[jax.random.permutation(jax.random.fold_in(own, 1), rows)]
    offset_by = jax.random.randint(jax.random.fold_in(own, 2), (rows, 1), 0, top)
    return jnp.take_along_axis(listing, (jnp.arange(top)[None, :] + offset_by) % top, axis=1)


def portions_of(number_of, total, reach, lean, full):
    weights = [(1 << 20) // math.isqrt(rank ** lean) + 1 for rank in range(1, number_of + 1)]
    largest = reach if full else min(reach, max(-(-total // number_of), total * weights[0] // sum(weights)))
    least = 1 if total - largest >= number_of - 1 else 0
    given, surplus = [largest] + [least] * (number_of - 1), total - largest - least * (number_of - 1)
    while surplus > 0:
        movable = [i for i in range(1, number_of) if given[i] < largest] or [i for i in range(1, number_of) if given[i] < reach]
        mass, budget = sum([weights[i] for i in movable]), surplus
        for i in movable:
            addition = min(reach - given[i], max(1, budget * weights[i] // mass), surplus)
            given[i] = given[i] + addition
            surplus = surplus - addition
    return np.array(given)


def gaussian(stream_key, shape, width, most, pieces=(), kind=jnp.bfloat16):
    drawn = jax.random.normal(stream_key, shape, jnp.float32) * width
    if len(pieces) > 0:
        drawn = steps_of(stream_key, shape, pieces, -0.22, 0.18) * drawn
    return jnp.clip(drawn, min=-most, max=most).astype(kind)


def setup_inputs(seed: int = 0) -> dict:
    arg_keys = jax.random.split(jax.random.key(seed), 6)
    member_weights = gaussian(arg_keys[0], (MEMBERS, D, 2 * FW), D ** -0.5, 0.109375, ((0, 64), (1, 4)))
    cluster_ids = draw_cluster_ids(jax.random.fold_in(arg_keys[5], 71), 0)
    merge_counts = plant(jax.random.randint(arg_keys[2], (MEMBERS,), 1, 9), jax.random.fold_in(arg_keys[2], 1), 1, 8).astype(jnp.int32)
    tokens = gaussian(arg_keys[3], (TOKENS, D), 1.0, 6.0, ((0, 64),))
    routes_keys = jax.random.split(jax.random.fold_in(arg_keys[4], 1), TOKENS // TOK_DEV)
    routes_turns = jax.random.permutation(jax.random.fold_in(arg_keys[4], 3), TOKENS // TOK_DEV)
    routes = jax.vmap(lambda own, number: assign_block(jax.random.fold_in(arg_keys[4], 2), own, number, TOK_DEV, CLUSTERS, TOP, CAP, 2))(routes_keys, routes_turns).reshape((TOKENS, TOP))
    return dict(member_weights=member_weights, cluster_ids=cluster_ids, merge_counts=merge_counts, tokens=tokens, routes=routes)


def reference(member_weights, cluster_ids, merge_counts, tokens, routes):
    counts = merge_counts.astype(jnp.float32)

    def add_member(running, member):
        target = cluster_ids[member]
        member_block = lax.dynamic_index_in_dim(member_weights, member, 0, keepdims=False).astype(jnp.float32)
        current = lax.dynamic_index_in_dim(running, target, 0, keepdims=False)
        running = lax.dynamic_update_index_in_dim(running, current + counts[member] * member_block, target, 0)
        return running, None

    initial = jnp.zeros((CLUSTERS, D, 2 * FW), jnp.float32)
    summed, unused = lax.scan(add_member, initial, jnp.arange(MEMBERS, dtype=jnp.int32))
    totals = jax.ops.segment_sum(counts, cluster_ids, num_segments=CLUSTERS)
    merged = (summed / totals[:, None, None]).astype(jnp.bfloat16)
    quarter = FW // N_TENSOR
    relaid = merged.reshape(CLUSTERS, D, 2, N_TENSOR, quarter).transpose(0, 1, 3, 2, 4).reshape(CLUSTERS, D, 2 * FW)

    slot_count = N_EXPERT * CAP
    flat_routes = routes.reshape(-1)
    count_all = TOKENS * TOP
    ordering = jnp.argsort(flat_routes, stable=True).astype(jnp.int32)
    cluster_sizes = jax.ops.segment_sum(jnp.ones_like(flat_routes), flat_routes, num_segments=CLUSTERS).astype(jnp.int32)
    cluster_starts = (jnp.cumsum(cluster_sizes) - cluster_sizes).astype(jnp.int32)
    padded = jnp.concatenate([ordering, jnp.zeros((slot_count,), jnp.int32)])

    def per_cluster(outputs, target):
        picked = lax.dynamic_slice_in_dim(padded, cluster_starts[target], slot_count)
        is_valid = jnp.arange(slot_count, dtype=jnp.int32) < cluster_sizes[target]
        picked_rows = tokens[picked // TOP].astype(jnp.float32)
        merged_block = lax.dynamic_index_in_dim(merged, target, 0, keepdims=False).astype(jnp.float32)
        projected = jnp.dot(picked_rows, merged_block, precision=lax.Precision.HIGHEST)
        activated = jax.nn.silu(projected[:, :FW]) * projected[:, FW:]
        where_to = jnp.where(is_valid, picked, count_all).astype(jnp.int32)
        outputs = outputs.at[where_to].set(activated)
        return outputs, None

    blank_rows = jnp.zeros((count_all + 1, FW), jnp.float32)
    outputs, unused = lax.scan(per_cluster, blank_rows, jnp.arange(CLUSTERS, dtype=jnp.int32))
    hidden = outputs[:count_all].astype(jnp.bfloat16).reshape(TOKENS, TOP, FW)
    return relaid, hidden
```

```python
import jax
import jax.numpy as jnp
from jax import lax
from jax.experimental import pallas as pl
from jax.experimental.pallas import tpu as pltpu
from jax.sharding import PartitionSpec as P

MESH = pl.DeviceIdType.MESH
CHUNKS = ((0, 0, 1), (0, 1, 2), (1, 0, 3), (2, 0, 3), (3, 0, 3), (4, 0, 2), (4, 2, 1))
NC = len(CHUNKS)
NX, NY, NZ, NP, CAP = 4, 4, 8, 8, 16
W1, W2 = 256, 128
BF = jnp.bfloat16
F32 = jnp.float32


def chunk_shapes():
    ys, yr, xr, zr, bs, br = [], [], [], [], [], []
    for _, _, nj in CHUNKS:
        r = 16 * nj
        ys.append((NY, 2, 2, NZ, r, 128))
        yr.append((NY, 2, 2, NZ, r, 128))
        xr.append((NP, 2, NZ, r, 128))
        zr.append((NZ, NP, 2, r, 128))
        bs.append((NZ, NP, r, 128))
        br.append((NP, NZ, r, 128))
    return ys, yr, xr, zr, bs, br


S_Y, S_X, S_Z, S_BZ, S_BX = 0, NC, 2 * NC, 3 * NC, 4 * NC
S_TZ = 5 * NC
S_SZ, S_TX, S_TY, S_H1X, S_H1Z, S_H2X, S_H2Z = (S_TZ + i for i in range(1, 8))
NS = S_TZ + 8
L_RAW, L_TOK, L_OUT, L_F = 0, 3, 4, 9
NL = 10


def half_tiles(b, t):
    found = []
    for h in range(2):
        col = b * 128 + h * 64
        raw = t * 320 + col if col < 320 else 1280 + t * 320 + col - 320
        found.append((raw // 128, (raw // 64) % 2))
    return found


def kernel(idx_ref, wgt_ref, w_hbm, tok_hbm, sel_ref, f_hbm, *refs):
    out_hbm, hid_ref = refs[0], refs[1]
    yr, xr, br = refs[2:2 + NC], refs[2 + NC:2 + 2 * NC], refs[2 + 2 * NC:2 + 3 * NC]
    refs = refs[2 + 3 * NC:]
    ys, zr, bs = refs[:NC], refs[NC:2 * NC], refs[2 * NC:3 * NC]
    (raw, wv, tsrc, tz, sz, tsel, tok, acc, act1, act2, hx1, hx2, hz1, hz2, f_ref, ssem, rsem, lsem) = refs[3 * NC:]
    e = lax.axis_index("expert")
    y = lax.axis_index("tensor")
    x, z, k = e // 16, (e // 2) % 8, e % 2
    p = x * 2 + k

    def at_y(t):
        return {"expert": e, "tensor": t}

    def at_z(t):
        return {"expert": x * 16 + t * 2 + k, "tensor": y}

    def at_p(t):
        return {"expert": (t // 2) * 16 + z * 2 + t % 2, "tensor": y}

    groups = ((NY, y, at_y), (NP, p, at_p), (NZ, z, at_z))

    raw_loads = []
    for j in range(3):
        rows = pl.ds(j * 16, 16)
        c = pltpu.make_async_copy(w_hbm.at[:, :, :, rows, :], raw.at[:, :, :, rows, :], lsem.at[L_RAW + j])
        c.start()
        raw_loads.append(c)
        if j == 0:
            tok_load = pltpu.make_async_copy(tok_hbm.at[:, pl.ds(pl.multiple_of(y * 768, 128), 768)], tsrc, lsem.at[L_TOK])
            tok_load.start()
    f_load = pltpu.make_async_copy(f_hbm, f_ref, lsem.at[L_F])
    f_load.start()

    barrier = pltpu.get_barrier_semaphore()
    for n, me, at in groups:
        def greet(d, carry, n=n, me=me, at=at):
            pl.semaphore_signal(barrier, inc=1, device_id=at((me + d) % n), device_id_type=MESH)
            return carry
        lax.fori_loop(1, n, greet, 0)
    pl.semaphore_wait(barrier, NY + NP + NZ - 3)

    drains = []

    def exchange(group, stage, source, target, own=True):
        n, me, at = groups[group]
        if own:
            pltpu.make_async_copy(source(me), target(me), rsem.at[stage]).start()

        def send(d, carry):
            t = (me + d) % n
            pltpu.make_async_remote_copy(
                src_ref=source(t), dst_ref=target(me), send_sem=ssem.at[stage], recv_sem=rsem.at[stage],
                device_id=at(t), device_id_type=MESH,
            ).start()
            return carry

        lax.fori_loop(1, n, send, 0)

    def wait_all(stage, ref):
        pltpu.make_async_copy(ref, ref, rsem.at[stage]).wait()

    def drain(stage, ref):
        drains.append((stage, ref))

    def relayout(c):
        b, j0, nj = CHUNKS[c]
        rows = pl.ds(j0 * 16, nj * 16)
        lane = lax.broadcasted_iota(jnp.int32, (nj * 16, 128), 1)

        def one(i, carry):
            m, kk, zz = i // 16, (i // 8) % 2, i % 8
            for t in range(NY):
                (lo, lo_half), (hi, hi_half) = half_tiles(b, t)
                if lo == hi:
                    ys[c][t, m, kk, zz] = raw[m, kk, zz, rows, lo * 128:lo * 128 + 128]
                    continue
                low = raw[m, kk, zz, rows, lo * 128:lo * 128 + 128].astype(F32)
                high = raw[m, kk, zz, rows, hi * 128:hi * 128 + 128].astype(F32)
                if lo_half == 1:
                    low = pltpu.roll(low, 64, 1)
                if hi_half == 0:
                    high = pltpu.roll(high, 64, 1)
                ys[c][t, m, kk, zz] = jnp.where(lane < 64, low, high).astype(BF)
            return carry

        lax.fori_loop(0, 32, one, 0)

    def stage_y(c):
        exchange(0, S_Y + c, lambda t: ys[c].at[t], lambda s: yr[c].at[s])
        drain(S_Y + c, yr[c].at[pl.ds(0, 3)])

    def stage_x(c):
        wait_all(S_Y + c, yr[c])
        exchange(1, S_X + c, lambda t: yr[c].at[t // 2, :, t % 2], lambda s: xr[c].at[s])
        drain(S_X + c, xr[c].at[pl.ds(0, 7)])

    def stage_z(c):
        wait_all(S_X + c, xr[c])
        exchange(2, S_Z + c, lambda t: xr[c].at[:, :, t], lambda s: zr[c].at[s])
        drain(S_Z + c, zr[c].at[pl.ds(0, 7)])

    def stage_bz(c):
        wait_all(S_Z + c, zr[c])

        def one(i, carry):
            total = None
            for m in range(4):
                where = idx_ref[i * 4 + m]
                term = zr[c][where >> 4, (where >> 1) & 7, where & 1].astype(F32) * wgt_ref[i * 4 + m]
                total = term if total is None else total + term
            bs[c][i // 8, i % 8] = total.astype(BF)
            return carry

        lax.fori_loop(0, 64, one, 0)
        exchange(2, S_BZ + c, lambda t: bs[c].at[t], lambda s: br[c].at[:, s])
        drain(S_BZ + c, br[c].at[pl.ds(0, 7)])

    def stage_bx(c):
        b, j0, nj = CHUNKS[c]
        wait_all(S_BZ + c, br[c])
        exchange(1, S_BX + c, lambda t: br[c].at[t],
                 lambda s: wv.at[b, pl.ds(s * 8, 8), pl.ds(j0 * 16, nj * 16)])
        drain(S_BX + c, wv.at[b, pl.ds(0, 56), pl.ds(j0 * 16, nj * 16)])

    out_copies = []

    def served(c):
        b, j0, nj = CHUNKS[c]
        wait_all(S_BX + c, wv.at[b, :, pl.ds(j0 * 16, nj * 16)])
        if j0 + nj < 3:
            return
        copy = pltpu.make_async_copy(wv.at[b], out_hbm.at[:, :, pl.ds(b * 128, 128)], lsem.at[L_OUT + b])
        copy.start()
        out_copies.append(copy)

        def rows_of(i, carry):
            total = None
            for q in range(NY):
                lhs = tok[q, pl.ds(i * 4, 4)].reshape(512, 768)
                rhs = wv[b, pl.ds(q * 16, 16)].reshape(768, 128)
                part = jnp.dot(lhs, rhs, preferred_element_type=F32)
                total = part if total is None else total + part
            acc[pl.ds(i * 512, 512), b * 128:b * 128 + 128] = total
            return carry

        lax.fori_loop(0, 2, rows_of, 0)

    def silu_up(gate, up):
        return (gate / (1.0 + jnp.exp(-gate))) * up

    def activate_first():
        def one(i, carry):
            r = pl.ds(i * 128, 128)
            hidden = silu_up(acc[r, 0:192], acc[r, 320:512]).astype(BF)
            act1[i] = jnp.concatenate([hidden, jnp.zeros((128, 64), BF)], axis=1).reshape(8, 16, W1)
            return carry

        lax.fori_loop(0, 8, one, 0)

    def activate_second():
        def one(i, carry):
            r = pl.ds(i * 128, 128)
            act2[i] = silu_up(acc[r, 192:320], acc[r, 512:640]).astype(BF).reshape(8, 16, W2)
            return carry

        lax.fori_loop(0, 8, one, 0)

    def hidden_x(stage, act, hx):
        exchange(1, stage, lambda t: act.at[t], lambda s: hx.at[s])
        drain(stage, hx.at[pl.ds(0, 7)])

    def hidden_z(before, stage, hx, hz):
        wait_all(before, hx)
        exchange(2, stage, lambda t: hx.at[:, t], lambda s: hz.at[s])
        drain(stage, hz.at[pl.ds(0, 7)])

    def tokens_z():
        tok_load.wait()
        exchange(2, S_SZ, lambda t: sel_ref.at[t], lambda s: sz.at[s])
        exchange(2, S_TZ, lambda t: tsrc, lambda s: tz.at[s])
        drain(S_SZ, sz.at[pl.ds(0, 7)])
        drain(S_TZ, tz.at[pl.ds(0, 7)])

    def tokens_x():
        wait_all(S_SZ, sz)
        wait_all(S_TZ, tz)

        def one(i, carry):
            chosen = jnp.dot(sz[i][:, 0:64], tz[i], preferred_element_type=F32).astype(BF)
            tsel[:, i] = chosen.reshape(8, 16, 768)
            return carry

        lax.fori_loop(0, 8, one, 0)
        exchange(1, S_TX, lambda t: tsel.at[t], lambda s: tok.at[y, s])
        drain(S_TX, tsel.at[pl.ds(0, 7)])

    def tokens_y():
        wait_all(S_TX, tok.at[y])
        exchange(0, S_TY, lambda t: tok.at[y], lambda s: tok.at[s], own=False)
        drain(S_TY, tok.at[pl.ds(0, 3)])

    def tokens_done():
        wait_all(S_TY, tok.at[pl.ds(0, 3)])

    raw_loads[0].wait()
    relayout(0)
    stage_y(0)
    tokens_z()
    raw_loads[1].wait()
    raw_loads[2].wait()
    relayout(1)
    stage_x(0)
    stage_y(1)
    relayout(2)
    stage_z(0)
    stage_x(1)
    stage_y(2)
    tokens_x()
    relayout(3)
    stage_z(1)
    tokens_y()
    for c in range(NC):
        if c + 2 < NC:
            stage_x(c + 2)
        if c + 3 < NC:
            stage_y(c + 3)
        if c + 4 < NC:
            relayout(c + 4)
        stage_bz(c)
        if c + 2 < NC:
            stage_z(c + 2)
        if c >= 1:
            stage_bx(c - 1)
        if c == 2:
            tokens_done()
        if c >= 2:
            served(c - 2)
    f_load.wait()
    stage_bx(NC - 1)
    served(NC - 2)
    activate_first()
    hidden_x(S_H1X, act1, hx1)
    hidden_z(S_H1X, S_H1Z, hx1, hz1)
    served(NC - 1)
    activate_second()
    hidden_x(S_H2X, act2, hx2)
    hidden_z(S_H2X, S_H2Z, hx2, hz2)

    def finish(hz, width, keep, at):
        got = jnp.dot(f_ref[...], hz[...].reshape(1024, width), preferred_element_type=F32)
        hid_ref[:, :, at:at + keep] = got[:, 0:keep].reshape(64, 8, keep).astype(BF)

    wait_all(S_H1Z, hz1)
    finish(hz1, W1, 192, 0)
    wait_all(S_H2Z, hz2)
    finish(hz2, W2, 128, 192)
    for copy in out_copies:
        copy.wait()
    for stage, ref in drains:
        pltpu.make_async_copy(ref, ref, ssem.at[stage]).wait()


def on_device(member_weights, cluster_ids, merge_counts, tokens, routes):
    member_count = cluster_ids.shape[0]
    cluster_count = 64
    ids = cluster_ids
    same = ids[None, :] == ids[:, None]
    earlier = jnp.arange(member_count)[None, :] < jnp.arange(member_count)[:, None]
    place = jnp.sum(same & earlier, axis=1)
    zz, pp = jnp.meshgrid(jnp.arange(8), jnp.arange(8), indexing="ij")
    cluster_of = ((pp // 2) * 16 + zz * 2 + pp % 2).reshape(-1)
    member = jnp.arange(member_count, dtype=jnp.int32)
    owner = member // 2
    encoded = ((owner // 2) % 8) * 16 + ((owner // 16) * 2 + owner % 2) * 2 + member % 2
    hit = (ids[None, None, :] == cluster_of[:, None, None]) & (place[None, None, :] == jnp.arange(4)[None, :, None])
    index_table = jnp.sum(jnp.where(hit, encoded, 0), axis=2).astype(jnp.int32)
    count_table = jnp.sum(jnp.where(hit, merge_counts, 0), axis=2).astype(F32)
    weight_table = count_table / jnp.sum(count_table, axis=1, keepdims=True)

    token_count, top = routes.shape
    named = jnp.any(routes[None, :, :] == jnp.arange(cluster_count)[:, None, None], axis=2)
    before = jnp.arange(token_count)[:, None] < jnp.arange(token_count)[None, :]
    rank = jnp.dot(named.astype(BF), before.astype(BF), preferred_element_type=F32).astype(jnp.int32)
    tagged = jnp.where(named, rank, -1)
    tagged = tagged.reshape(4, 8, 2, token_count).transpose(1, 0, 2, 3).reshape(cluster_count, 1, token_count)
    chosen = (tagged == jnp.arange(CAP)[None, :, None]).astype(BF).reshape(8, 128, token_count)
    selection = jnp.pad(chosen, ((0, 0), (0, 0), (0, 128 - token_count)))
    my_rank = jnp.sum(jnp.where(routes[:, :, None] == jnp.arange(cluster_count), rank.T[:, None, :], 0), axis=2)
    slot = ((routes // 2) % 8) * 128 + ((routes // 16) * 2 + routes % 2) * CAP + my_rank
    finder = (slot.reshape(-1, 1) == jnp.arange(1024)[None, :]).astype(BF)

    ys, yr, xr, zr, bs, br = chunk_shapes()
    hbm = pl.BlockSpec(memory_space=pltpu.HBM)
    vmem = pl.BlockSpec(memory_space=pltpu.VMEM)
    smem = pl.BlockSpec(memory_space=pltpu.SMEM)
    outs = [jax.ShapeDtypeStruct((64, 48, 640), BF), jax.ShapeDtypeStruct((64, 8, 320), BF)]
    outs += [jax.ShapeDtypeStruct(s, BF) for s in yr + xr + br]
    scratch = [pltpu.VMEM(s, BF) for s in ys + zr + bs]
    scratch += [
        pltpu.VMEM((2, 2, 8, 48, 2560), BF),
        pltpu.VMEM((5, 64, 48, 128), BF),
        pltpu.VMEM((64, 768), BF),
        pltpu.VMEM((8, 64, 768), BF),
        pltpu.VMEM((8, 128, 128), BF),
        pltpu.VMEM((8, 8, 16, 768), BF),
        pltpu.VMEM((4, 8, 8, 16, 768), BF),
        pltpu.VMEM((1024, 640), F32),
        pltpu.VMEM((8, 8, 16, W1), BF),
        pltpu.VMEM((8, 8, 16, W2), BF),
        pltpu.VMEM((8, 8, 16, W1), BF),
        pltpu.VMEM((8, 8, 16, W2), BF),
        pltpu.VMEM((8, 8, 16, W1), BF),
        pltpu.VMEM((8, 8, 16, W2), BF),
        pltpu.VMEM((512, 1024), BF),
        pltpu.SemaphoreType.DMA((NS,)),
        pltpu.SemaphoreType.DMA((NS,)),
        pltpu.SemaphoreType.DMA((NL,)),
    ]
    results = pl.pallas_call(
        kernel,
        out_shape=outs,
        in_specs=[smem, smem, hbm, hbm, vmem, hbm],
        out_specs=[hbm, vmem] + [hbm] * (3 * NC),
        scratch_shapes=scratch,
        compiler_params=pltpu.CompilerParams(collective_id=0, has_side_effects=True, vmem_limit_bytes=60 * 1024 * 1024),
    )(
        index_table.reshape(-1), weight_table.reshape(-1), member_weights.reshape(2, 2, 8, 48, 2560), tokens,
        selection, finder,
    )
    return results[0].reshape(1, 3072, 640), results[1]


def solution(mesh):
    return jax.shard_map(
        on_device,
        mesh=mesh,
        in_specs=(P("expert", "tensor", None), P(), P(), P("expert", None), P("expert", None)),
        out_specs=(P("expert", None, "tensor"), P("expert", None, "tensor")),
        check_vma=False,
    )
```

```python
import jax
import jax.numpy as jnp
from jax import lax
from jax.experimental import pallas as pl
from jax.experimental.pallas import tpu as pltpu
from jax.sharding import PartitionSpec as P

MESH = pl.DeviceIdType.MESH
CHUNKS = ((0, 0, 1), (0, 1, 1), (0, 2, 1), (1, 0, 3), (2, 0, 3), (3, 0, 3), (4, 0, 1), (4, 1, 1), (4, 2, 1))
ORDER = (
    "TZ", "Y0", "Y1", "X0", "Y2", "Y3", "X1", "Z0", "TX", "X2", "Z1", "E0", "E1", "Y4", "B0", "Y8", "Y7", "X3", "Z2",
    "B1", "E2", "Z3", "X4", "Y6", "X8", "Z4", "G1", "Y5", "X5", "B2", "E3", "X7", "TY", "Z5", "E4", "E5", "B3", "B4",
    "B5", "G2", "Z7", "G0", "Z8", "G3", "G4", "X6", "S1", "S2", "E7", "Z6", "G5", "S0", "S3", "E8", "B7", "E6", "H",
    "B8", "B6", "G7", "G8", "I", "G6", "S4", "J", "K",
)
NC = len(CHUNKS)
NX, NY, NZ, NP, CAP = 4, 4, 8, 8, 16
W1, W2 = 256, 128
BF = jnp.bfloat16
F32 = jnp.float32


def chunk_shapes():
    ys, yr, xr, zr, es, er, bs, br = [], [], [], [], [], [], [], []
    for _, _, nj in CHUNKS:
        r = 16 * nj
        ys.append((NY, 2, 2, NZ, r, 128))
        yr.append((NY, 2, 2, NZ, r, 128))
        xr.append((NP, 2, NZ, r, 128))
        zr.append((2, 4, NP, 2, r, 128))
        es.append((2, 4, NP, r, 128))
        er.append((2, 4, NP, r, 128))
        bs.append((2, 4, NP, r, 128))
        br.append((NP, NZ, r, 128))
    return ys, yr, xr, zr, es, er, bs, br


S_Y, S_X, S_Z, S_E, S_BZ, S_BX = 0, NC, 2 * NC, 3 * NC, 4 * NC, 5 * NC
S_TZ = 6 * NC
S_SZ, S_TX, S_TY, S_H1X, S_H1Z, S_H2X, S_H2Z = (S_TZ + i for i in range(1, 8))
NS = S_TZ + 8
L_RAW, L_TOK, L_OUT, L_F = 0, 3, 4, 9
NL = 10


def half_tiles(b, t):
    found = []
    for h in range(2):
        col = b * 128 + h * 64
        raw = t * 320 + col if col < 320 else 1280 + t * 320 + col - 320
        found.append((raw // 128, (raw // 64) % 2))
    return found


def kernel(idx_ref, wgt_ref, w_hbm, tok_hbm, sel_ref, f_hbm, *refs):
    out_hbm, hid_ref = refs[0], refs[1]
    yr, xr, br = refs[2:2 + NC], refs[2 + NC:2 + 2 * NC], refs[2 + 2 * NC:2 + 3 * NC]
    refs = refs[2 + 3 * NC:]
    ys, zr, es, er, bs = (refs[i * NC:(i + 1) * NC] for i in range(5))
    (raw, wv, tsrc, tz, sz, tsel, tok, acc, act1, act2, hx1, hx2, hz1, hz2, f_ref, ssem, rsem, lsem) = refs[5 * NC:]
    e = lax.axis_index("expert")
    y = lax.axis_index("tensor")
    x, z, k = e // 16, (e // 2) % 8, e % 2
    p = x * 2 + k

    def at_y(t):
        return {"expert": e, "tensor": t}

    def at_z(t):
        return {"expert": x * 16 + t * 2 + k, "tensor": y}

    def at_p(t):
        return {"expert": (t // 2) * 16 + z * 2 + t % 2, "tensor": y}

    groups = ((NY, y, at_y), (NP, p, at_p), (NZ, z, at_z))

    raw_loads = []
    for j in range(3):
        rows = pl.ds(j * 16, 16)
        c = pltpu.make_async_copy(w_hbm.at[:, :, :, rows, :], raw.at[:, :, :, rows, :], lsem.at[L_RAW + j])
        c.start()
        raw_loads.append(c)
        if j == 0:
            tok_load = pltpu.make_async_copy(tok_hbm.at[:, pl.ds(pl.multiple_of(y * 768, 128), 768)], tsrc, lsem.at[L_TOK])
            tok_load.start()
    f_load = pltpu.make_async_copy(f_hbm, f_ref, lsem.at[L_F])
    f_load.start()

    barrier = pltpu.get_barrier_semaphore()
    for n, me, at in groups:
        def greet(d, carry, n=n, me=me, at=at):
            pl.semaphore_signal(barrier, inc=1, device_id=at((me + d) % n), device_id_type=MESH)
            return carry
        lax.fori_loop(1, n, greet, 0)
    pl.semaphore_wait(barrier, NY + NP + NZ - 3)

    drains = []

    def exchange(group, stage, source, target, own=True):
        n, me, at = groups[group]
        if own:
            pltpu.make_async_copy(source(me), target(me), rsem.at[stage]).start()

        def send(d, carry):
            t = (me + d) % n
            pltpu.make_async_remote_copy(
                src_ref=source(t), dst_ref=target(me), send_sem=ssem.at[stage], recv_sem=rsem.at[stage],
                device_id=at(t), device_id_type=MESH,
            ).start()
            return carry

        lax.fori_loop(1, n, send, 0)

    def wait_all(stage, ref):
        pltpu.make_async_copy(ref, ref, rsem.at[stage]).wait()

    def drain(stage, ref):
        drains.append((stage, ref))

    def relayout(c):
        b, j0, nj = CHUNKS[c]
        rows = pl.ds(j0 * 16, nj * 16)
        lane = lax.broadcasted_iota(jnp.int32, (nj * 16, 128), 1)

        def one(i, carry):
            m, kk, zz = i // 16, (i // 8) % 2, i % 8
            for t in range(NY):
                (lo, lo_half), (hi, hi_half) = half_tiles(b, t)
                if lo == hi:
                    ys[c][t, m, kk, zz] = raw[m, kk, zz, rows, lo * 128:lo * 128 + 128]
                    continue
                low = raw[m, kk, zz, rows, lo * 128:lo * 128 + 128].astype(F32)
                high = raw[m, kk, zz, rows, hi * 128:hi * 128 + 128].astype(F32)
                if lo_half == 1:
                    low = pltpu.roll(low, 64, 1)
                if hi_half == 0:
                    high = pltpu.roll(high, 64, 1)
                ys[c][t, m, kk, zz] = jnp.where(lane < 64, low, high).astype(BF)
            return carry

        lax.fori_loop(0, 32, one, 0)

    def stage_y(c):
        exchange(0, S_Y + c, lambda t: ys[c].at[t], lambda s: yr[c].at[s])
        drain(S_Y + c, yr[c].at[pl.ds(0, 3)])

    def stage_x(c):
        wait_all(S_Y + c, yr[c])
        exchange(1, S_X + c, lambda t: yr[c].at[t // 2, :, t % 2], lambda s: xr[c].at[s])
        drain(S_X + c, xr[c].at[pl.ds(0, 7)])

    def send_z(stage, source, target, there):
        pltpu.make_async_remote_copy(
            src_ref=source, dst_ref=target, send_sem=ssem.at[stage], recv_sem=rsem.at[stage],
            device_id=at_z(there), device_id_type=MESH,
        ).start()

    def stage_z(c):
        wait_all(S_X + c, xr[c])
        pltpu.make_async_copy(xr[c].at[:, :, z], zr[c].at[0, 0], rsem.at[S_Z + c]).start()
        pltpu.make_async_copy(xr[c].at[:, :, (z + 7) % 8], zr[c].at[1, 0], rsem.at[S_Z + c]).start()

        def send(o, carry):
            send_z(S_Z + c, xr[c].at[:, :, (z + o) % 8], zr[c].at[0, o], (z + o) % 8)
            send_z(S_Z + c, xr[c].at[:, :, (z + 7 - o) % 8], zr[c].at[1, o], (z + 8 - o) % 8)
            return carry

        lax.fori_loop(1, 4, send, 0)
        drain(S_Z + c, zr[c].at[:, pl.ds(0, 3)])

    def weighted(c, role, entry):
        total = None
        for m in range(4):
            where = idx_ref[entry + m]
            term = zr[c][role, where >> 4, (where >> 1) & 7, where & 1].astype(F32) * wgt_ref[entry + m]
            total = term if total is None else total + term
        return total

    def stage_e(c):
        wait_all(S_Z + c, zr[c])

        def one(i, carry):
            es[c][i // 32, (i // 8) % 4, i % 8] = weighted(c, i // 32, i * 4).astype(BF)
            return carry

        lax.fori_loop(0, 64, one, 0)
        send_z(S_E + c, es[c].at[0], er[c].at[1], (z + 1) % 8)
        send_z(S_E + c, es[c].at[1], er[c].at[0], (z + 7) % 8)
        drain(S_E + c, er[c])

    def stage_bz(c):
        wait_all(S_E + c, er[c])

        def one(i, carry):
            role, plane, owner = i // 32, (i // 8) % 4, i % 8
            total = weighted(c, role, 256 + i * 4) + er[c][role, plane, owner].astype(F32)
            bs[c][role, plane, owner] = total.astype(BF)
            return carry

        lax.fori_loop(0, 64, one, 0)
        low = (z + 7) % 8
        pltpu.make_async_copy(bs[c].at[0, 0], br[c].at[:, z], rsem.at[S_BZ + c]).start()
        pltpu.make_async_copy(bs[c].at[1, 0], br[c].at[:, low], rsem.at[S_BZ + c]).start()

        def send(o, carry):
            send_z(S_BZ + c, bs[c].at[0, o], br[c].at[:, z], (z + 8 - o) % 8)
            send_z(S_BZ + c, bs[c].at[1, o], br[c].at[:, low], (z + o) % 8)
            return carry

        lax.fori_loop(1, 4, send, 0)
        drain(S_BZ + c, br[c].at[pl.ds(0, 6)])

    def stage_bx(c):
        b, j0, nj = CHUNKS[c]
        wait_all(S_BZ + c, br[c])
        exchange(1, S_BX + c, lambda t: br[c].at[t],
                 lambda s: wv.at[b, pl.ds(s * 8, 8), pl.ds(j0 * 16, nj * 16)])
        drain(S_BX + c, wv.at[b, pl.ds(0, 56), pl.ds(j0 * 16, nj * 16)])

    out_copies = []

    ready = []

    def served(b):
        if not ready:
            tokens_done()
            ready.append(True)
        for c, (block, j0, nj) in enumerate(CHUNKS):
            if block == b:
                wait_all(S_BX + c, wv.at[b, :, pl.ds(j0 * 16, nj * 16)])
        copy = pltpu.make_async_copy(wv.at[b], out_hbm.at[:, :, pl.ds(b * 128, 128)], lsem.at[L_OUT + b])
        copy.start()
        out_copies.append(copy)

        def rows_of(i, carry):
            total = None
            for q in range(NY):
                lhs = tok[q, pl.ds(i * 4, 4)].reshape(512, 768)
                rhs = wv[b, pl.ds(q * 16, 16)].reshape(768, 128)
                part = jnp.dot(lhs, rhs, preferred_element_type=F32)
                total = part if total is None else total + part
            acc[pl.ds(i * 512, 512), b * 128:b * 128 + 128] = total
            return carry

        lax.fori_loop(0, 2, rows_of, 0)

    def silu_up(gate, up):
        return (gate / (1.0 + jnp.exp(-gate))) * up

    def activate_first():
        def one(i, carry):
            r = pl.ds(i * 128, 128)
            hidden = silu_up(acc[r, 0:192], acc[r, 320:512]).astype(BF)
            act1[i] = jnp.concatenate([hidden, jnp.zeros((128, 64), BF)], axis=1).reshape(8, 16, W1)
            return carry

        lax.fori_loop(0, 8, one, 0)

    def activate_second():
        def one(i, carry):
            r = pl.ds(i * 128, 128)
            act2[i] = silu_up(acc[r, 192:320], acc[r, 512:640]).astype(BF).reshape(8, 16, W2)
            return carry

        lax.fori_loop(0, 8, one, 0)

    def hidden_x(stage, act, hx):
        exchange(1, stage, lambda t: act.at[t], lambda s: hx.at[s])
        drain(stage, hx.at[pl.ds(0, 7)])

    def hidden_z(before, stage, hx, hz):
        wait_all(before, hx)
        exchange(2, stage, lambda t: hx.at[:, t], lambda s: hz.at[s])
        drain(stage, hz.at[pl.ds(0, 7)])

    def tokens_z():
        tok_load.wait()
        exchange(2, S_SZ, lambda t: sel_ref.at[t], lambda s: sz.at[s])
        exchange(2, S_TZ, lambda t: tsrc, lambda s: tz.at[s])
        drain(S_SZ, sz.at[pl.ds(0, 7)])
        drain(S_TZ, tz.at[pl.ds(0, 7)])

    def tokens_x():
        wait_all(S_SZ, sz)
        wait_all(S_TZ, tz)

        def one(i, carry):
            chosen = jnp.dot(sz[i][:, 0:64], tz[i], preferred_element_type=F32).astype(BF)
            tsel[:, i] = chosen.reshape(8, 16, 768)
            return carry

        lax.fori_loop(0, 8, one, 0)
        exchange(1, S_TX, lambda t: tsel.at[t], lambda s: tok.at[y, s])
        drain(S_TX, tsel.at[pl.ds(0, 7)])

    def tokens_y():
        wait_all(S_TX, tok.at[y])
        exchange(0, S_TY, lambda t: tok.at[y], lambda s: tok.at[s], own=False)
        drain(S_TY, tok.at[pl.ds(0, 3)])

    def tokens_done():
        wait_all(S_TY, tok.at[pl.ds(0, 3)])

    loaded = set()

    def first(c):
        b, j0, nj = CHUNKS[c]
        for j in range(j0, j0 + nj):
            if j not in loaded:
                loaded.add(j)
                raw_loads[j].wait()
        relayout(c)
        stage_y(c)

    def third():
        activate_first()
        hidden_x(S_H1X, act1, hx1)

    def fourth():
        activate_second()
        hidden_x(S_H2X, act2, hx2)

    stages = {"Y": first, "X": stage_x, "Z": stage_z, "E": stage_e, "B": stage_bz, "G": stage_bx, "S": served}
    once = {
        "TZ": tokens_z, "TX": tokens_x, "TY": tokens_y, "H": third, "J": fourth,
        "I": lambda: hidden_z(S_H1X, S_H1Z, hx1, hz1), "K": lambda: hidden_z(S_H2X, S_H2Z, hx2, hz2),
    }
    for step in ORDER:
        if step in once:
            once[step]()
        else:
            stages[step[0]](int(step[1:]))
    f_load.wait()

    def finish(hz, width, keep, at):
        got = jnp.dot(f_ref[...], hz[...].reshape(1024, width), preferred_element_type=F32)
        hid_ref[:, :, at:at + keep] = got[:, 0:keep].reshape(64, 8, keep).astype(BF)

    wait_all(S_H1Z, hz1)
    finish(hz1, W1, 192, 0)
    wait_all(S_H2Z, hz2)
    finish(hz2, W2, 128, 192)
    for copy in out_copies:
        copy.wait()
    for stage, ref in drains:
        pltpu.make_async_copy(ref, ref, ssem.at[stage]).wait()


def on_device(member_weights, cluster_ids, merge_counts, tokens, routes):
    member_count = cluster_ids.shape[0]
    cluster_count = 64
    z = (lax.axis_index("expert") // 2) % 8
    same = cluster_ids[None, :] == cluster_ids[:, None]
    member = jnp.arange(member_count, dtype=jnp.int32)
    place = jnp.sum(same & (member[None, :] < member[:, None]), axis=1)
    weight = merge_counts.astype(F32) / jnp.sum(jnp.where(same, merge_counts[None, :], 0), axis=1).astype(F32)
    entry = jnp.arange(512, dtype=jnp.int32)
    own, role, i, p, m = entry // 256, (entry // 128) % 2, (entry // 32) % 4, (entry // 4) % 8, entry % 4
    plane = jnp.where(role == 0, jnp.where(own == 1, z - i, z + 1 + i), jnp.where(own == 1, z + i, z - 1 - i)) % 8
    cluster_of = (p // 2) * 16 + plane * 2 + p % 2
    owner = member // 2
    away = (z - (owner // 2) % 8) % 8
    away = jnp.where(role[:, None] == 0, away[None, :], ((8 - away) % 8)[None, :])
    hit = (cluster_ids[None, :] == cluster_of[:, None]) & (place[None, :] == m[:, None]) & (away < 4)
    inside = ((owner // 16) * 2 + owner % 2) * 2 + member % 2
    index_table = jnp.sum(jnp.where(hit, away * 16 + inside[None, :], 0), axis=1).astype(jnp.int32)
    weight_table = jnp.sum(jnp.where(hit, weight[None, :], 0.0), axis=1)

    token_count, top = routes.shape
    named = jnp.any(routes[None, :, :] == jnp.arange(cluster_count)[:, None, None], axis=2)
    before = jnp.arange(token_count)[:, None] < jnp.arange(token_count)[None, :]
    rank = jnp.dot(named.astype(BF), before.astype(BF), preferred_element_type=F32).astype(jnp.int32)
    tagged = jnp.where(named, rank, -1)
    tagged = tagged.reshape(4, 8, 2, token_count).transpose(1, 0, 2, 3).reshape(cluster_count, 1, token_count)
    chosen = (tagged == jnp.arange(CAP)[None, :, None]).astype(BF).reshape(8, 128, token_count)
    selection = jnp.pad(chosen, ((0, 0), (0, 0), (0, 128 - token_count)))
    my_rank = jnp.sum(jnp.where(routes[:, :, None] == jnp.arange(cluster_count), rank.T[:, None, :], 0), axis=2)
    slot = ((routes // 2) % 8) * 128 + ((routes // 16) * 2 + routes % 2) * CAP + my_rank
    finder = (slot.reshape(-1, 1) == jnp.arange(1024)[None, :]).astype(BF)

    ys, yr, xr, zr, es, er, bs, br = chunk_shapes()
    hbm = pl.BlockSpec(memory_space=pltpu.HBM)
    vmem = pl.BlockSpec(memory_space=pltpu.VMEM)
    smem = pl.BlockSpec(memory_space=pltpu.SMEM)
    outs = [jax.ShapeDtypeStruct((64, 48, 640), BF), jax.ShapeDtypeStruct((64, 8, 320), BF)]
    outs += [jax.ShapeDtypeStruct(s, BF) for s in yr + xr + br]
    scratch = [pltpu.VMEM(s, BF) for s in ys + zr + es + er + bs]
    scratch += [
        pltpu.VMEM((2, 2, 8, 48, 2560), BF),
        pltpu.VMEM((5, 64, 48, 128), BF),
        pltpu.VMEM((64, 768), BF),
        pltpu.VMEM((8, 64, 768), BF),
        pltpu.VMEM((8, 128, 128), BF),
        pltpu.VMEM((8, 8, 16, 768), BF),
        pltpu.VMEM((4, 8, 8, 16, 768), BF),
        pltpu.VMEM((1024, 640), F32),
        pltpu.VMEM((8, 8, 16, W1), BF),
        pltpu.VMEM((8, 8, 16, W2), BF),
        pltpu.VMEM((8, 8, 16, W1), BF),
        pltpu.VMEM((8, 8, 16, W2), BF),
        pltpu.VMEM((8, 8, 16, W1), BF),
        pltpu.VMEM((8, 8, 16, W2), BF),
        pltpu.VMEM((512, 1024), BF),
        pltpu.SemaphoreType.DMA((NS,)),
        pltpu.SemaphoreType.DMA((NS,)),
        pltpu.SemaphoreType.DMA((NL,)),
    ]
    results = pl.pallas_call(
        kernel,
        out_shape=outs,
        in_specs=[smem, smem, hbm, hbm, vmem, hbm],
        out_specs=[hbm, vmem] + [hbm] * (3 * NC),
        scratch_shapes=scratch,
        compiler_params=pltpu.CompilerParams(collective_id=0, has_side_effects=True, vmem_limit_bytes=60 * 1024 * 1024),
    )(
        index_table, weight_table, member_weights.reshape(2, 2, 8, 48, 2560), tokens,
        selection, finder,
    )
    return results[0].reshape(1, 3072, 640), results[1]


def solution(mesh):
    return jax.shard_map(
        on_device,
        mesh=mesh,
        in_specs=(P("expert", "tensor", None), P(), P(), P("expert", None), P("expert", None)),
        out_specs=(P("expert", None, "tensor"), P("expert", None, "tensor")),
        check_vma=False,
    )
```

```python
import jax
import jax.numpy as jnp
from jax import lax
from jax.experimental import pallas as pl
from jax.experimental.pallas import tpu as pltpu
from jax.sharding import PartitionSpec as P

MESH = pl.DeviceIdType.MESH
CHUNKS = ((0, 0, 1), (0, 1, 1), (0, 2, 1), (1, 0, 3), (2, 0, 3), (3, 0, 3), (4, 0, 1), (4, 1, 1), (4, 2, 1))
ORDER = (
    "Y1", "TZ", "Y2", "Y7", "X1", "X2", "Y0", "Z1", "Y5", "Y3", "X7", "Z2", "M", "E1", "Y4", "X0", "Z7", "Z0", "B1",
    "X5", "Y8", "E2", "E7", "E0", "Z5", "X3", "Y6", "G1", "X4", "Z3", "E5", "B2", "Z4", "TX", "TY", "T", "E3", "X8",
    "B5", "B0", "G2", "E4", "B3", "X6", "Z8", "G0", "B4", "G5", "S3", "G3", "S0", "Z6", "G4", "E8", "S1", "B7", "E6",
    "B8", "S2", "H", "B6", "G7", "G8", "I", "G6", "S4", "J", "K",
)
NC = len(CHUNKS)
NX, NY, NZ, NP, CAP = 4, 4, 8, 8, 16
W1, W2 = 256, 128
BF = jnp.bfloat16
F32 = jnp.float32


def chunk_shapes():
    ys, yr, xr, zr, es, er, bs, br = [], [], [], [], [], [], [], []
    for _, _, nj in CHUNKS:
        r = 16 * nj
        ys.append((NY, 2, 2, NZ, r, 128))
        yr.append((NY, 2, 2, NZ, r, 128))
        xr.append((NP, 2, NZ, r, 128))
        zr.append((2, 4, NP, 2, r, 128))
        es.append((2, 4, NP, r, 128))
        er.append((2, 4, NP, r, 128))
        bs.append((2, 4, NP, r, 128))
        br.append((NP, NZ, r, 128))
    return ys, yr, xr, zr, es, er, bs, br


S_Y, S_X, S_Z, S_E, S_BZ, S_BX = 0, NC, 2 * NC, 3 * NC, 4 * NC, 5 * NC
S_TZ = 6 * NC
S_SZ, S_TX, S_TY, S_H1X, S_H1Z, S_H2X, S_H2Z = (S_TZ + i for i in range(1, 8))
NS = S_TZ + 8
L_RAW, L_TOK, L_OUT, L_TAB = 0, 3, 4, 9
NL = 11


def half_tiles(b, t):
    found = []
    for h in range(2):
        col = b * 128 + h * 64
        raw = t * 320 + col if col < 320 else 1280 + t * 320 + col - 320
        found.append((raw // 128, (raw // 64) % 2))
    return found


def kernel(ids_ref, cnt_ref, routes_ref, w_hbm, tok_hbm, *refs):
    out_hbm, hid_ref = refs[0], refs[1]
    yr, xr, br = refs[2:2 + NC], refs[2 + NC:2 + 2 * NC], refs[2 + 2 * NC:2 + 3 * NC]
    refs = refs[2 + 3 * NC:]
    ys, zr, es, er, bs = (refs[i * NC:(i + 1) * NC] for i in range(5))
    (raw, wv, tsrc, tz, sz, tsel, tok, acc, act1, act2, hx1, hx2, hz1, hz2, f_ref,
     f_tmp, sel_ref, idx_vmem, wgt_vmem, idx_ref, wgt_ref, ssem, rsem, lsem) = refs[5 * NC:]
    e = lax.axis_index("expert")
    y = lax.axis_index("tensor")
    x, z, k = e // 16, (e // 2) % 8, e % 2
    p = x * 2 + k

    def at_y(t):
        return {"expert": e, "tensor": t}

    def at_z(t):
        return {"expert": x * 16 + t * 2 + k, "tensor": y}

    def at_p(t):
        return {"expert": (t // 2) * 16 + z * 2 + t % 2, "tensor": y}

    groups = ((NY, y, at_y), (NP, p, at_p), (NZ, z, at_z))

    raw_loads = []
    for j in range(3):
        rows = pl.ds(j * 16, 16)
        c = pltpu.make_async_copy(w_hbm.at[:, :, :, rows, :], raw.at[:, :, :, rows, :], lsem.at[L_RAW + j])
        c.start()
        raw_loads.append(c)
        if j == 0:
            tok_load = pltpu.make_async_copy(tok_hbm.at[:, pl.ds(pl.multiple_of(y * 768, 128), 768)], tsrc, lsem.at[L_TOK])
            tok_load.start()
    barrier = pltpu.get_barrier_semaphore()
    for n, me, at in groups:
        def greet(d, carry, n=n, me=me, at=at):
            pl.semaphore_signal(barrier, inc=1, device_id=at((me + d) % n), device_id_type=MESH)
            return carry
        lax.fori_loop(1, n, greet, 0)
    def iota(rows, columns, axis):
        return lax.broadcasted_iota(jnp.int32, (rows, columns), axis)

    drains = []

    def exchange(group, stage, source, target, own=True):
        n, me, at = groups[group]
        if own:
            pltpu.make_async_copy(source(me), target(me), rsem.at[stage]).start()

        def send(d, carry):
            t = (me + d) % n
            pltpu.make_async_remote_copy(
                src_ref=source(t), dst_ref=target(me), send_sem=ssem.at[stage], recv_sem=rsem.at[stage],
                device_id=at(t), device_id_type=MESH,
            ).start()
            return carry

        lax.fori_loop(1, n, send, 0)

    def wait_all(stage, ref):
        pltpu.make_async_copy(ref, ref, rsem.at[stage]).wait()

    def drain(stage, ref):
        drains.append((stage, ref))

    def relayout(c):
        b, j0, nj = CHUNKS[c]
        rows = pl.ds(j0 * 16, nj * 16)
        lane = lax.broadcasted_iota(jnp.int32, (nj * 16, 128), 1)

        def one(i, carry):
            m, kk, zz = i // 16, (i // 8) % 2, i % 8
            for t in range(NY):
                (lo, lo_half), (hi, hi_half) = half_tiles(b, t)
                if lo == hi:
                    ys[c][t, m, kk, zz] = raw[m, kk, zz, rows, lo * 128:lo * 128 + 128]
                    continue
                low = raw[m, kk, zz, rows, lo * 128:lo * 128 + 128].astype(F32)
                high = raw[m, kk, zz, rows, hi * 128:hi * 128 + 128].astype(F32)
                if lo_half == 1:
                    low = pltpu.roll(low, 64, 1)
                if hi_half == 0:
                    high = pltpu.roll(high, 64, 1)
                ys[c][t, m, kk, zz] = jnp.where(lane < 64, low, high).astype(BF)
            return carry

        lax.fori_loop(0, 32, one, 0)

    def stage_y(c):
        exchange(0, S_Y + c, lambda t: ys[c].at[t], lambda s: yr[c].at[s])
        drain(S_Y + c, yr[c].at[pl.ds(0, 3)])

    def stage_x(c):
        wait_all(S_Y + c, yr[c])
        exchange(1, S_X + c, lambda t: yr[c].at[t // 2, :, t % 2], lambda s: xr[c].at[s])
        drain(S_X + c, xr[c].at[pl.ds(0, 7)])

    def send_z(stage, source, target, there):
        pltpu.make_async_remote_copy(
            src_ref=source, dst_ref=target, send_sem=ssem.at[stage], recv_sem=rsem.at[stage],
            device_id=at_z(there), device_id_type=MESH,
        ).start()

    def stage_z(c):
        wait_all(S_X + c, xr[c])
        pltpu.make_async_copy(xr[c].at[:, :, z], zr[c].at[0, 0], rsem.at[S_Z + c]).start()
        pltpu.make_async_copy(xr[c].at[:, :, (z + 7) % 8], zr[c].at[1, 0], rsem.at[S_Z + c]).start()

        def send(o, carry):
            send_z(S_Z + c, xr[c].at[:, :, (z + o) % 8], zr[c].at[0, o], (z + o) % 8)
            send_z(S_Z + c, xr[c].at[:, :, (z + 7 - o) % 8], zr[c].at[1, o], (z + 8 - o) % 8)
            return carry

        lax.fori_loop(1, 4, send, 0)
        drain(S_Z + c, zr[c].at[:, pl.ds(0, 3)])

    def weighted(c, role, entry):
        total = None
        for m in range(4):
            where = idx_ref[0, entry + m]
            term = zr[c][role, (where >> 4) & 3, (where >> 1) & 7, where & 1].astype(F32) * wgt_ref[0, entry + m]
            total = term if total is None else total + term
        return total

    def stage_e(c):
        wait_all(S_Z + c, zr[c])

        def one(i, carry):
            es[c][i // 32, (i // 8) % 4, i % 8] = weighted(c, i // 32, i * 4).astype(BF)
            return carry

        lax.fori_loop(0, 64, one, 0)
        send_z(S_E + c, es[c].at[0], er[c].at[1], (z + 1) % 8)
        send_z(S_E + c, es[c].at[1], er[c].at[0], (z + 7) % 8)
        drain(S_E + c, er[c])

    def stage_bz(c):
        wait_all(S_E + c, er[c])

        def one(i, carry):
            role, plane, owner = i // 32, (i // 8) % 4, i % 8
            total = weighted(c, role, 256 + i * 4) + er[c][role, plane, owner].astype(F32)
            bs[c][role, plane, owner] = total.astype(BF)
            return carry

        lax.fori_loop(0, 64, one, 0)
        low = (z + 7) % 8
        pltpu.make_async_copy(bs[c].at[0, 0], br[c].at[:, z], rsem.at[S_BZ + c]).start()
        pltpu.make_async_copy(bs[c].at[1, 0], br[c].at[:, low], rsem.at[S_BZ + c]).start()

        def send(o, carry):
            send_z(S_BZ + c, bs[c].at[0, o], br[c].at[:, z], (z + 8 - o) % 8)
            send_z(S_BZ + c, bs[c].at[1, o], br[c].at[:, low], (z + o) % 8)
            return carry

        lax.fori_loop(1, 4, send, 0)
        drain(S_BZ + c, br[c].at[pl.ds(0, 6)])

    def stage_bx(c):
        b, j0, nj = CHUNKS[c]
        wait_all(S_BZ + c, br[c])
        exchange(1, S_BX + c, lambda t: br[c].at[t],
                 lambda s: wv.at[b, pl.ds(s * 8, 8), pl.ds(j0 * 16, nj * 16)])
        drain(S_BX + c, wv.at[b, pl.ds(0, 56), pl.ds(j0 * 16, nj * 16)])

    out_copies = []

    ready = []

    def served(b):
        if not ready:
            tokens_done()
            ready.append(True)
        for c, (block, j0, nj) in enumerate(CHUNKS):
            if block == b:
                wait_all(S_BX + c, wv.at[b, :, pl.ds(j0 * 16, nj * 16)])
        copy = pltpu.make_async_copy(wv.at[b], out_hbm.at[:, :, pl.ds(b * 128, 128)], lsem.at[L_OUT + b])
        copy.start()
        out_copies.append(copy)

        def rows_of(i, carry):
            total = None
            for q in range(NY):
                lhs = tok[q, pl.ds(i * 4, 4)].reshape(512, 768)
                rhs = wv[b, pl.ds(q * 16, 16)].reshape(768, 128)
                part = jnp.dot(lhs, rhs, preferred_element_type=F32)
                total = part if total is None else total + part
            acc[pl.ds(i * 512, 512), b * 128:b * 128 + 128] = total
            return carry

        lax.fori_loop(0, 2, rows_of, 0)

    def silu_up(gate, up):
        return (gate / (1.0 + jnp.exp(-gate))) * up

    def activate_first():
        def one(i, carry):
            r = pl.ds(i * 128, 128)
            hidden = silu_up(acc[r, 0:192], acc[r, 320:512]).astype(BF)
            act1[i] = jnp.concatenate([hidden, jnp.zeros((128, 64), BF)], axis=1).reshape(8, 16, W1)
            return carry

        lax.fori_loop(0, 8, one, 0)

    def activate_second():
        def one(i, carry):
            r = pl.ds(i * 128, 128)
            act2[i] = silu_up(acc[r, 192:320], acc[r, 512:640]).astype(BF).reshape(8, 16, W2)
            return carry

        lax.fori_loop(0, 8, one, 0)

    def hidden_x(stage, act, hx):
        exchange(1, stage, lambda t: act.at[t], lambda s: hx.at[s])
        drain(stage, hx.at[pl.ds(0, 7)])

    def hidden_z(before, stage, hx, hz):
        wait_all(before, hx)
        exchange(2, stage, lambda t: hx.at[:, t], lambda s: hz.at[s])
        drain(stage, hz.at[pl.ds(0, 7)])

    def tokens_z():
        tok_load.wait()
        exchange(2, S_SZ, lambda t: sel_ref.at[t], lambda s: sz.at[s])
        exchange(2, S_TZ, lambda t: tsrc, lambda s: tz.at[s])
        drain(S_SZ, sz.at[pl.ds(0, 7)])
        drain(S_TZ, tz.at[pl.ds(0, 7)])

    def tokens_x():
        wait_all(S_SZ, sz)
        wait_all(S_TZ, tz)
        repeat = jnp.where((iota(128, 16, 0) >> 4) == iota(128, 16, 1), 1.0, 0.0).astype(BF)
        slot = (iota(128, 128, 0) & 15).astype(F32)

        def one(i, carry):
            ranks = jnp.dot(repeat, sz[i], preferred_element_type=F32)
            pick = jnp.where(ranks == slot, 1.0, 0.0)[:, 0:64].astype(BF)
            chosen = jnp.dot(pick, tz[i], preferred_element_type=F32).astype(BF)
            tsel[:, i] = chosen.reshape(8, 16, 768)
            return carry

        lax.fori_loop(0, 8, one, 0)
        exchange(1, S_TX, lambda t: tsel.at[t], lambda s: tok.at[y, s])
        drain(S_TX, tsel.at[pl.ds(0, 7)])

    def tokens_y():
        wait_all(S_TX, tok.at[y])
        exchange(0, S_TY, lambda t: tok.at[y], lambda s: tok.at[s], own=False)
        drain(S_TY, tok.at[pl.ds(0, 3)])

    def tokens_done():
        wait_all(S_TY, tok.at[pl.ds(0, 3)])

    def merge_tables():
        ids, counts = ids_ref[...], cnt_ref[...]
        row, column = iota(128, 128, 0), iota(128, 128, 1)
        ids_down = jnp.sum(jnp.where(row == column, ids, 0), axis=1, keepdims=True)
        counts_down = jnp.sum(jnp.where(row == column, counts, 0), axis=1, keepdims=True)
        same = ids_down == ids
        place = jnp.sum(jnp.where(same & (column < row), 1, 0), axis=1, keepdims=True)
        total = jnp.sum(jnp.where(same, counts, 0), axis=1, keepdims=True)
        weight = counts_down.astype(F32) / total.astype(F32)
        member = iota(128, 512, 0)
        owner = member >> 1
        plane_of = (owner >> 1) & 7
        inside = ((owner >> 4) * 2 + (owner & 1)) * 2 + (member & 1)
        entry = iota(128, 512, 1)
        own, role, i, q, m = entry >> 8, (entry >> 7) & 1, (entry >> 5) & 3, (entry >> 2) & 7, entry & 3
        plane = jnp.where(role == 0, jnp.where(own == 1, z - i, z + 1 + i), jnp.where(own == 1, z + i, z - 1 - i)) & 7
        cluster = (q >> 1) * 16 + plane * 2 + (q & 1)
        away = jnp.where(role == 0, z - plane_of, plane_of - z) & 7
        hit = (ids_down == cluster) & (place == m) & (away < 4)
        idx_vmem[...] = jnp.sum(jnp.where(hit, away * 16 + inside, 0), axis=0, keepdims=True)
        wgt_vmem[...] = jnp.sum(jnp.where(hit, weight, 0.0), axis=0, keepdims=True)
        pltpu.make_async_copy(idx_vmem, idx_ref, lsem.at[L_TAB]).start()
        pltpu.make_async_copy(wgt_vmem, wgt_ref, lsem.at[L_TAB + 1]).start()

    def merge_tables_done():
        pltpu.make_async_copy(idx_vmem, idx_ref, lsem.at[L_TAB]).wait()
        pltpu.make_async_copy(wgt_vmem, wgt_ref, lsem.at[L_TAB + 1]).wait()

    def slot_ranks():
        routes = routes_ref[...]
        hits = [jnp.where(routes[:, j:j + 1] == iota(64, 64, 1), 1.0, 0.0) for j in range(8)]
        named = sum(hits[1:], hits[0])
        lower = jnp.where(iota(64, 64, 1) < iota(64, 64, 0), 1.0, 0.0).astype(BF)
        rank = jnp.dot(lower, named.astype(BF), preferred_element_type=F32)
        return routes, hits, named, rank

    def select_tokens():
        routes, hits, named, rank = slot_ranks()
        tagged = jnp.where(named > 0.0, rank, -1.0)
        tagged = jnp.concatenate([tagged, jnp.full((64, 64), -1.0, F32)], axis=0).astype(BF)
        unit = jnp.where(iota(64, 64, 0) == iota(64, 64, 1), 1.0, 0.0).astype(BF)
        across = lax.dot_general(unit, tagged, (((1,), (1,)), ((), ())), preferred_element_type=F32).astype(BF)
        row = iota(128, 64, 0)
        cluster = ((row & 15) >> 1) * 16 + (row >> 4) * 2 + (row & 1)
        spread = jnp.where(cluster == iota(128, 64, 1), 1.0, 0.0).astype(BF)
        sel_ref[...] = jnp.dot(spread, across, preferred_element_type=F32).astype(BF).reshape(8, 16, 128)

    def find_slots():
        routes, hits, named, rank = slot_ranks()
        for j in range(8):
            mine = jnp.sum(hits[j] * rank, axis=1, keepdims=True).astype(jnp.int32)
            r = routes[:, j:j + 1]
            slot = ((r >> 1) & 7) * 128 + ((r >> 4) * 2 + (r & 1)) * CAP + mine
            f_tmp[j * 64:j * 64 + 64, :] = jnp.where(slot == iota(64, 1024, 1), 1.0, 0.0).astype(BF)

        def one(i, carry):
            row = iota(128, 512, 0) + i * 128
            order = jnp.where(iota(128, 512, 1) == (row & 7) * 64 + (row >> 3), 1.0, 0.0).astype(BF)
            f_ref[pl.ds(i * 128, 128), :] = jnp.dot(order, f_tmp[...], preferred_element_type=F32).astype(BF)
            return carry

        lax.fori_loop(0, 4, one, 0)

    loaded = set()
    early = set()

    def first(c):
        b, j0, nj = CHUNKS[c]
        for j in range(j0, j0 + nj):
            if j not in loaded:
                loaded.add(j)
                raw_loads[j].wait()
        if c not in early:
            relayout(c)
        stage_y(c)

    def third():
        activate_first()
        hidden_x(S_H1X, act1, hx1)

    def fourth():
        activate_second()
        hidden_x(S_H2X, act2, hx2)

    stages = {"Y": first, "X": stage_x, "Z": stage_z, "E": stage_e, "B": stage_bz, "G": stage_bx, "S": served}
    once = {
        "M": merge_tables_done, "T": find_slots, "TZ": tokens_z, "TX": tokens_x, "TY": tokens_y, "H": third, "J": fourth,
        "I": lambda: hidden_z(S_H1X, S_H1Z, hx1, hz1), "K": lambda: hidden_z(S_H2X, S_H2Z, hx2, hz2),
    }
    merge_tables()
    select_tokens()
    raw_loads[0].wait()
    loaded.add(0)
    relayout(0)
    early.add(0)
    pl.semaphore_wait(barrier, NY + NP + NZ - 3)
    for step in ORDER:
        if step in once:
            once[step]()
        else:
            stages[step[0]](int(step[1:]))

    def finish(hz, width, keep, at):
        got = jnp.dot(f_ref[...], hz[...].reshape(1024, width), preferred_element_type=F32)
        hid_ref[:, :, at:at + keep] = got[:, 0:keep].reshape(64, 8, keep).astype(BF)

    wait_all(S_H1Z, hz1)
    finish(hz1, W1, 192, 0)
    wait_all(S_H2Z, hz2)
    finish(hz2, W2, 128, 192)
    for copy in out_copies:
        copy.wait()
    for stage, ref in drains:
        pltpu.make_async_copy(ref, ref, ssem.at[stage]).wait()


def on_device(member_weights, cluster_ids, merge_counts, tokens, routes):
    ys, yr, xr, zr, es, er, bs, br = chunk_shapes()
    hbm = pl.BlockSpec(memory_space=pltpu.HBM)
    vmem = pl.BlockSpec(memory_space=pltpu.VMEM)
    outs = [jax.ShapeDtypeStruct((64, 48, 640), BF), jax.ShapeDtypeStruct((64, 8, 320), BF)]
    outs += [jax.ShapeDtypeStruct(s, BF) for s in yr + xr + br]
    scratch = [pltpu.VMEM(s, BF) for s in ys + zr + es + er + bs]
    scratch += [
        pltpu.VMEM((2, 2, 8, 48, 2560), BF),
        pltpu.VMEM((5, 64, 48, 128), BF),
        pltpu.VMEM((64, 768), BF),
        pltpu.VMEM((8, 64, 768), BF),
        pltpu.VMEM((8, 16, 128), BF),
        pltpu.VMEM((8, 8, 16, 768), BF),
        pltpu.VMEM((4, 8, 8, 16, 768), BF),
        pltpu.VMEM((1024, 640), F32),
        pltpu.VMEM((8, 8, 16, W1), BF),
        pltpu.VMEM((8, 8, 16, W2), BF),
        pltpu.VMEM((8, 8, 16, W1), BF),
        pltpu.VMEM((8, 8, 16, W2), BF),
        pltpu.VMEM((8, 8, 16, W1), BF),
        pltpu.VMEM((8, 8, 16, W2), BF),
        pltpu.VMEM((512, 1024), BF),
        pltpu.VMEM((512, 1024), BF),
        pltpu.VMEM((8, 16, 128), BF),
        pltpu.VMEM((1, 512), jnp.int32),
        pltpu.VMEM((1, 512), F32),
        pltpu.SMEM((1, 512), jnp.int32),
        pltpu.SMEM((1, 512), F32),
        pltpu.SemaphoreType.DMA((NS,)),
        pltpu.SemaphoreType.DMA((NS,)),
        pltpu.SemaphoreType.DMA((NL,)),
    ]
    results = pl.pallas_call(
        kernel,
        out_shape=outs,
        in_specs=[vmem, vmem, vmem, hbm, hbm],
        out_specs=[hbm, vmem] + [hbm] * (3 * NC),
        scratch_shapes=scratch,
        compiler_params=pltpu.CompilerParams(collective_id=0, has_side_effects=True, vmem_limit_bytes=60 * 1024 * 1024),
    )(
        cluster_ids.reshape(1, -1), merge_counts.reshape(1, -1), routes, member_weights.reshape(2, 2, 8, 48, 2560), tokens,
    )
    return results[0].reshape(1, 3072, 640), results[1]


def solution(mesh):
    return jax.shard_map(
        on_device,
        mesh=mesh,
        in_specs=(P("expert", "tensor", None), P(), P(), P("expert", None), P("expert", None)),
        out_specs=(P("expert", None, "tensor"), P("expert", None, "tensor")),
        check_vma=False,
    )
```

```python
import jax
import jax.numpy as jnp
from jax import lax
from jax.experimental import pallas as pl
from jax.experimental.pallas import tpu as pltpu
from jax.sharding import PartitionSpec as P

MESH = pl.DeviceIdType.MESH
CHUNKS = ((0, 0, 1), (0, 1, 1), (0, 2, 1), (1, 0, 3), (2, 0, 3), (3, 0, 3), (4, 0, 1), (4, 1, 1), (4, 2, 1))
ORDER = (
    "Y1", "TZ", "Y2", "Y7", "X1", "X2", "Y0", "Z1", "Y5", "Y3", "X7", "Z2", "M", "E1", "Y4", "X0", "Z7", "Z0", "B1",
    "X5", "Y8", "E2", "E7", "E0", "Z5", "X3", "Y6", "G1", "X4", "Z3", "E5", "B2", "Z4", "TX", "TY", "T", "E3", "X8",
    "B5", "B0", "G2", "E4", "B3", "X6", "Z8", "G0", "B4", "G5", "S3", "G3", "S0", "Z6", "G4", "E8", "S1", "B7", "E6",
    "B8", "S2", "H", "B6", "G7", "G8", "I", "G6", "S4", "J", "K",
)
NC = len(CHUNKS)
NX, NY, NZ, NP, CAP = 4, 4, 8, 8, 16
W1, W2 = 256, 128
BF = jnp.bfloat16
F32 = jnp.float32


def chunk_shapes():
    ys, yr, xr, zr, es, er, bs, br = [], [], [], [], [], [], [], []
    for _, _, nj in CHUNKS:
        r = 16 * nj
        ys.append((NY, 2, 2, NZ, r, 128))
        yr.append((NY, 2, 2, NZ, r, 128))
        xr.append((NP, 2, NZ, r, 128))
        zr.append((2, 4, NP, 2, r, 128))
        es.append((2, 4, NP, r, 128))
        er.append((2, 4, NP, r, 128))
        bs.append((2, 4, NP, r, 128))
        br.append((NP, NZ, r, 128))
    return ys, yr, xr, zr, es, er, bs, br


S_Y, S_X, S_Z, S_E, S_BZ, S_BX = 0, NC, 2 * NC, 3 * NC, 4 * NC, 5 * NC
S_TZ = 6 * NC
S_SZ, S_TX, S_TY, S_H1X, S_H1Z, S_H1B, S_H2X, S_H2Z = (S_TZ + i for i in range(1, 9))
NS = S_TZ + 9
L_RAW, L_TOK, L_OUT, L_TAB, L_F = 0, 3, 4, 9, 11
NL = 12


def half_tiles(b, t):
    found = []
    for h in range(2):
        col = b * 128 + h * 64
        raw = t * 320 + col if col < 320 else 1280 + t * 320 + col - 320
        found.append((raw // 128, (raw // 64) % 2))
    return found


def kernel(ids_ref, cnt_ref, routes_ref, w_hbm, tok_hbm, *refs):
    out_hbm, f_hbm, hz1, hz1b, hz2 = refs[:5]
    yr, xr, br = (refs[5 + i * NC:5 + (i + 1) * NC] for i in range(3))
    refs = refs[5 + 3 * NC:]
    ys, zr, es, er, bs = (refs[i * NC:(i + 1) * NC] for i in range(5))
    (raw, wv, tsrc, tz, sz, tsel, tok, acc, act1, act2, hx1, hx2, pack, f_ref,
     f_tmp, sel_ref, idx_vmem, wgt_vmem, idx_ref, wgt_ref, ssem, rsem, lsem) = refs[5 * NC:]
    e = lax.axis_index("expert")
    y = lax.axis_index("tensor")
    x, z, k = e // 16, (e // 2) % 8, e % 2
    p = x * 2 + k

    def at_y(t):
        return {"expert": e, "tensor": t}

    def at_z(t):
        return {"expert": x * 16 + t * 2 + k, "tensor": y}

    def at_p(t):
        return {"expert": (t // 2) * 16 + z * 2 + t % 2, "tensor": y}

    groups = ((NY, y, at_y), (NP, p, at_p), (NZ, z, at_z))

    raw_loads = []
    for j in range(3):
        rows = pl.ds(j * 16, 16)
        c = pltpu.make_async_copy(w_hbm.at[:, :, :, rows, :], raw.at[:, :, :, rows, :], lsem.at[L_RAW + j])
        c.start()
        raw_loads.append(c)
        if j == 0:
            tok_load = pltpu.make_async_copy(tok_hbm.at[:, pl.ds(pl.multiple_of(y * 768, 128), 768)], tsrc, lsem.at[L_TOK])
            tok_load.start()
    barrier = pltpu.get_barrier_semaphore()
    for n, me, at in groups:
        def greet(d, carry, n=n, me=me, at=at):
            pl.semaphore_signal(barrier, inc=1, device_id=at((me + d) % n), device_id_type=MESH)
            return carry
        lax.fori_loop(1, n, greet, 0)
    def iota(rows, columns, axis):
        return lax.broadcasted_iota(jnp.int32, (rows, columns), axis)

    drains = []

    def exchange(group, stage, source, target, own=True):
        n, me, at = groups[group]
        if own:
            pltpu.make_async_copy(source(me), target(me), rsem.at[stage]).start()

        def send(d, carry):
            t = (me + d) % n
            pltpu.make_async_remote_copy(
                src_ref=source(t), dst_ref=target(me), send_sem=ssem.at[stage], recv_sem=rsem.at[stage],
                device_id=at(t), device_id_type=MESH,
            ).start()
            return carry

        lax.fori_loop(1, n, send, 0)

    def wait_all(stage, ref):
        pltpu.make_async_copy(ref, ref, rsem.at[stage]).wait()

    def drain(stage, ref):
        drains.append((stage, ref))

    def relayout(c):
        b, j0, nj = CHUNKS[c]
        rows = pl.ds(j0 * 16, nj * 16)
        lane = lax.broadcasted_iota(jnp.int32, (nj * 16, 128), 1)

        def one(i, carry):
            m, kk, zz = i // 16, (i // 8) % 2, i % 8
            for t in range(NY):
                (lo, lo_half), (hi, hi_half) = half_tiles(b, t)
                if lo == hi:
                    ys[c][t, m, kk, zz] = raw[m, kk, zz, rows, lo * 128:lo * 128 + 128]
                    continue
                low = raw[m, kk, zz, rows, lo * 128:lo * 128 + 128].astype(F32)
                high = raw[m, kk, zz, rows, hi * 128:hi * 128 + 128].astype(F32)
                if lo_half == 1:
                    low = pltpu.roll(low, 64, 1)
                if hi_half == 0:
                    high = pltpu.roll(high, 64, 1)
                ys[c][t, m, kk, zz] = jnp.where(lane < 64, low, high).astype(BF)
            return carry

        lax.fori_loop(0, 32, one, 0)

    def stage_y(c):
        exchange(0, S_Y + c, lambda t: ys[c].at[t], lambda s: yr[c].at[s])
        drain(S_Y + c, yr[c].at[pl.ds(0, 3)])

    def stage_x(c):
        wait_all(S_Y + c, yr[c])
        exchange(1, S_X + c, lambda t: yr[c].at[t // 2, :, t % 2], lambda s: xr[c].at[s])
        drain(S_X + c, xr[c].at[pl.ds(0, 7)])

    def send_z(stage, source, target, there):
        pltpu.make_async_remote_copy(
            src_ref=source, dst_ref=target, send_sem=ssem.at[stage], recv_sem=rsem.at[stage],
            device_id=at_z(there), device_id_type=MESH,
        ).start()

    def stage_z(c):
        wait_all(S_X + c, xr[c])
        pltpu.make_async_copy(xr[c].at[:, :, z], zr[c].at[0, 0], rsem.at[S_Z + c]).start()
        pltpu.make_async_copy(xr[c].at[:, :, (z + 7) % 8], zr[c].at[1, 0], rsem.at[S_Z + c]).start()

        def send(o, carry):
            send_z(S_Z + c, xr[c].at[:, :, (z + o) % 8], zr[c].at[0, o], (z + o) % 8)
            send_z(S_Z + c, xr[c].at[:, :, (z + 7 - o) % 8], zr[c].at[1, o], (z + 8 - o) % 8)
            return carry

        lax.fori_loop(1, 4, send, 0)
        drain(S_Z + c, zr[c].at[:, pl.ds(0, 3)])

    def weighted(c, role, entry):
        total = None
        for m in range(4):
            where = idx_ref[0, entry + m]
            term = zr[c][role, (where >> 4) & 3, (where >> 1) & 7, where & 1].astype(F32) * wgt_ref[0, entry + m]
            total = term if total is None else total + term
        return total

    def stage_e(c):
        wait_all(S_Z + c, zr[c])

        def one(i, carry):
            es[c][i // 32, (i // 8) % 4, i % 8] = weighted(c, i // 32, i * 4).astype(BF)
            return carry

        lax.fori_loop(0, 64, one, 0)
        send_z(S_E + c, es[c].at[0], er[c].at[1], (z + 1) % 8)
        send_z(S_E + c, es[c].at[1], er[c].at[0], (z + 7) % 8)
        drain(S_E + c, er[c])

    def stage_bz(c):
        wait_all(S_E + c, er[c])

        def one(i, carry):
            role, plane, owner = i // 32, (i // 8) % 4, i % 8
            total = weighted(c, role, 256 + i * 4) + er[c][role, plane, owner].astype(F32)
            bs[c][role, plane, owner] = total.astype(BF)
            return carry

        lax.fori_loop(0, 64, one, 0)
        low = (z + 7) % 8
        pltpu.make_async_copy(bs[c].at[0, 0], br[c].at[:, z], rsem.at[S_BZ + c]).start()
        pltpu.make_async_copy(bs[c].at[1, 0], br[c].at[:, low], rsem.at[S_BZ + c]).start()

        def send(o, carry):
            send_z(S_BZ + c, bs[c].at[0, o], br[c].at[:, z], (z + 8 - o) % 8)
            send_z(S_BZ + c, bs[c].at[1, o], br[c].at[:, low], (z + o) % 8)
            return carry

        lax.fori_loop(1, 4, send, 0)
        drain(S_BZ + c, br[c].at[pl.ds(0, 6)])

    def stage_bx(c):
        b, j0, nj = CHUNKS[c]
        wait_all(S_BZ + c, br[c])
        exchange(1, S_BX + c, lambda t: br[c].at[t],
                 lambda s: wv.at[b, pl.ds(s * 8, 8), pl.ds(j0 * 16, nj * 16)])
        drain(S_BX + c, wv.at[b, pl.ds(0, 56), pl.ds(j0 * 16, nj * 16)])

    out_copies = []

    ready = []

    def served(b):
        if not ready:
            tokens_done()
            ready.append(True)
        for c, (block, j0, nj) in enumerate(CHUNKS):
            if block == b:
                wait_all(S_BX + c, wv.at[b, :, pl.ds(j0 * 16, nj * 16)])
        copy = pltpu.make_async_copy(wv.at[b], out_hbm.at[b], lsem.at[L_OUT + b])
        copy.start()
        out_copies.append(copy)

        def rows_of(i, carry):
            total = None
            for q in range(NY):
                lhs = tok[q, pl.ds(i * 4, 4)].reshape(512, 768)
                rhs = wv[b, pl.ds(q * 16, 16)].reshape(768, 128)
                part = jnp.dot(lhs, rhs, preferred_element_type=F32)
                total = part if total is None else total + part
            acc[pl.ds(i * 512, 512), b * 128:b * 128 + 128] = total
            return carry

        lax.fori_loop(0, 2, rows_of, 0)

    def silu_up(gate, up):
        return (gate / (1.0 + jnp.exp(-gate))) * up

    def activate_first():
        def one(i, carry):
            r = pl.ds(i * 128, 128)
            hidden = silu_up(acc[r, 0:192], acc[r, 320:512]).astype(BF)
            act1[i] = jnp.concatenate([hidden, jnp.zeros((128, 64), BF)], axis=1).reshape(8, 16, W1)
            return carry

        lax.fori_loop(0, 8, one, 0)

    def activate_second():
        def one(i, carry):
            r = pl.ds(i * 128, 128)
            act2[i] = silu_up(acc[r, 192:320], acc[r, 512:640]).astype(BF).reshape(8, 16, W2)
            return carry

        lax.fori_loop(0, 8, one, 0)

    def hidden_x(stage, act, hx):
        exchange(1, stage, lambda t: act.at[t], lambda s: hx.at[s])
        drain(stage, hx.at[pl.ds(0, 7)])

    def hidden_z_first():
        wait_all(S_H1X, hx1)
        lanes = pl.ds(0, 128)
        exchange(2, S_H1Z, lambda t: hx1.at[:, t, :, lanes], lambda s: hz1.at[s])
        drain(S_H1Z, hz1.at[pl.ds(0, 7)])

        def one(i, carry):
            t, q = i // 4, i % 4
            pack[t, q] = jnp.concatenate([hx1[q, t, :, 128:192], hx1[q + 4, t, :, 128:192]], axis=1)
            return carry

        lax.fori_loop(0, 32, one, 0)
        exchange(2, S_H1B, lambda t: pack.at[t], lambda s: hz1b.at[s])
        drain(S_H1B, hz1b.at[pl.ds(0, 7)])

    def hidden_z_second():
        wait_all(S_H2X, hx2)
        exchange(2, S_H2Z, lambda t: hx2.at[:, t], lambda s: hz2.at[s])
        drain(S_H2Z, hz2.at[pl.ds(0, 7)])

    def tokens_z():
        tok_load.wait()
        exchange(2, S_SZ, lambda t: sel_ref.at[t], lambda s: sz.at[s])
        exchange(2, S_TZ, lambda t: tsrc, lambda s: tz.at[s])
        drain(S_SZ, sz.at[pl.ds(0, 7)])
        drain(S_TZ, tz.at[pl.ds(0, 7)])

    def tokens_x():
        wait_all(S_SZ, sz)
        wait_all(S_TZ, tz)
        repeat = jnp.where((iota(128, 16, 0) >> 4) == iota(128, 16, 1), 1.0, 0.0).astype(BF)
        slot = (iota(128, 128, 0) & 15).astype(F32)

        def one(i, carry):
            ranks = jnp.dot(repeat, sz[i], preferred_element_type=F32)
            pick = jnp.where(ranks == slot, 1.0, 0.0)[:, 0:64].astype(BF)
            chosen = jnp.dot(pick, tz[i], preferred_element_type=F32).astype(BF)
            tsel[:, i] = chosen.reshape(8, 16, 768)
            return carry

        lax.fori_loop(0, 8, one, 0)
        exchange(1, S_TX, lambda t: tsel.at[t], lambda s: tok.at[y, s])
        drain(S_TX, tsel.at[pl.ds(0, 7)])

    def tokens_y():
        wait_all(S_TX, tok.at[y])
        exchange(0, S_TY, lambda t: tok.at[y], lambda s: tok.at[s], own=False)
        drain(S_TY, tok.at[pl.ds(0, 3)])

    def tokens_done():
        wait_all(S_TY, tok.at[pl.ds(0, 3)])

    def merge_tables():
        ids, counts = ids_ref[...], cnt_ref[...]
        row, column = iota(128, 128, 0), iota(128, 128, 1)
        ids_down = jnp.sum(jnp.where(row == column, ids, 0), axis=1, keepdims=True)
        counts_down = jnp.sum(jnp.where(row == column, counts, 0), axis=1, keepdims=True)
        same = ids_down == ids
        place = jnp.sum(jnp.where(same & (column < row), 1, 0), axis=1, keepdims=True)
        total = jnp.sum(jnp.where(same, counts, 0), axis=1, keepdims=True)
        weight = counts_down.astype(F32) / total.astype(F32)
        member = iota(128, 512, 0)
        owner = member >> 1
        plane_of = (owner >> 1) & 7
        inside = ((owner >> 4) * 2 + (owner & 1)) * 2 + (member & 1)
        entry = iota(128, 512, 1)
        own, role, i, q, m = entry >> 8, (entry >> 7) & 1, (entry >> 5) & 3, (entry >> 2) & 7, entry & 3
        plane = jnp.where(role == 0, jnp.where(own == 1, z - i, z + 1 + i), jnp.where(own == 1, z + i, z - 1 - i)) & 7
        cluster = (q >> 1) * 16 + plane * 2 + (q & 1)
        away = jnp.where(role == 0, z - plane_of, plane_of - z) & 7
        hit = (ids_down == cluster) & (place == m) & (away < 4)
        idx_vmem[...] = jnp.sum(jnp.where(hit, away * 16 + inside, 0), axis=0, keepdims=True)
        wgt_vmem[...] = jnp.sum(jnp.where(hit, weight, 0.0), axis=0, keepdims=True)
        pltpu.make_async_copy(idx_vmem, idx_ref, lsem.at[L_TAB]).start()
        pltpu.make_async_copy(wgt_vmem, wgt_ref, lsem.at[L_TAB + 1]).start()

    def merge_tables_done():
        pltpu.make_async_copy(idx_vmem, idx_ref, lsem.at[L_TAB]).wait()
        pltpu.make_async_copy(wgt_vmem, wgt_ref, lsem.at[L_TAB + 1]).wait()

    def slot_ranks():
        unit = jnp.where(iota(64, 64, 0) == iota(64, 64, 1), 1.0, 0.0).astype(BF)
        turned = routes_ref[...].astype(F32).astype(BF)
        routes = lax.dot_general(unit, turned, (((1,), (1,)), ((), ())), preferred_element_type=F32).astype(jnp.int32)
        hits = [jnp.where(routes[:, j:j + 1] == iota(64, 64, 1), 1.0, 0.0) for j in range(8)]
        named = sum(hits[1:], hits[0])
        lower = jnp.where(iota(64, 64, 1) < iota(64, 64, 0), 1.0, 0.0).astype(BF)
        rank = jnp.dot(lower, named.astype(BF), preferred_element_type=F32)
        return routes, hits, named, rank

    def select_tokens():
        routes, hits, named, rank = slot_ranks()
        tagged = jnp.where(named > 0.0, rank, -1.0)
        tagged = jnp.concatenate([tagged, jnp.full((64, 64), -1.0, F32)], axis=0).astype(BF)
        unit = jnp.where(iota(64, 64, 0) == iota(64, 64, 1), 1.0, 0.0).astype(BF)
        across = lax.dot_general(unit, tagged, (((1,), (1,)), ((), ())), preferred_element_type=F32).astype(BF)
        row = iota(128, 64, 0)
        cluster = ((row & 15) >> 1) * 16 + (row >> 4) * 2 + (row & 1)
        spread = jnp.where(cluster == iota(128, 64, 1), 1.0, 0.0).astype(BF)
        sel_ref[...] = jnp.dot(spread, across, preferred_element_type=F32).astype(BF).reshape(8, 16, 128)

    def find_slots():
        routes, hits, named, rank = slot_ranks()
        for j in range(8):
            mine = jnp.sum(hits[j] * rank, axis=1, keepdims=True).astype(jnp.int32)
            r = routes[:, j:j + 1]
            slot = ((r >> 1) & 7) * 128 + ((r >> 4) * 2 + (r & 1)) * CAP + mine
            f_tmp[j * 64:j * 64 + 64, :] = jnp.where(slot == iota(64, 1024, 1), 1.0, 0.0).astype(BF)

        def one(i, carry):
            row = iota(128, 512, 0) + i * 128
            order = jnp.where(iota(128, 512, 1) == (row & 7) * 64 + (row >> 3), 1.0, 0.0).astype(BF)
            f_ref[pl.ds(i * 128, 128), :] = jnp.dot(order, f_tmp[...], preferred_element_type=F32).astype(BF)
            return carry

        lax.fori_loop(0, 4, one, 0)
        copy = pltpu.make_async_copy(f_ref, f_hbm, lsem.at[L_F])
        copy.start()
        out_copies.append(copy)

    loaded = set()
    early = set()

    def first(c):
        b, j0, nj = CHUNKS[c]
        for j in range(j0, j0 + nj):
            if j not in loaded:
                loaded.add(j)
                raw_loads[j].wait()
        if c not in early:
            relayout(c)
        stage_y(c)

    def third():
        activate_first()
        hidden_x(S_H1X, act1, hx1)

    def fourth():
        activate_second()
        hidden_x(S_H2X, act2, hx2)

    stages = {"Y": first, "X": stage_x, "Z": stage_z, "E": stage_e, "B": stage_bz, "G": stage_bx, "S": served}
    once = {
        "M": merge_tables_done, "T": find_slots, "TZ": tokens_z, "TX": tokens_x, "TY": tokens_y, "H": third, "J": fourth,
        "I": hidden_z_first, "K": hidden_z_second,
    }
    merge_tables()
    select_tokens()
    opening = int(next(step for step in ORDER if step[0] == "Y")[1:])
    for j in range(CHUNKS[opening][1], CHUNKS[opening][1] + CHUNKS[opening][2]):
        raw_loads[j].wait()
        loaded.add(j)
    relayout(opening)
    early.add(opening)
    pl.semaphore_wait(barrier, NY + NP + NZ - 3)
    for step in ORDER:
        if step in once:
            once[step]()
        else:
            stages[step[0]](int(step[1:]))

    wait_all(S_H1Z, hz1)
    wait_all(S_H1B, hz1b)
    wait_all(S_H2Z, hz2)
    for copy in out_copies:
        copy.wait()
    for stage, ref in drains:
        pltpu.make_async_copy(ref, ref, ssem.at[stage]).wait()


def place_results(blocks, f_ref, first_ref, tail_ref, last_ref, out_hbm, hid_ref, held, load_sem, store_sem):
    loads, stores = [], []
    for b in range(5):
        loads.append(pltpu.make_async_copy(blocks.at[b], held.at[b], load_sem.at[b]))
        stores.append(pltpu.make_async_copy(held.at[b], out_hbm.at[:, :, pl.ds(b * 128, 128)], store_sem.at[b]))
        loads[b].start()

    def find(rows):
        return jnp.dot(f_ref[...], rows, preferred_element_type=F32)

    tail = tail_ref[...]
    tail = jnp.concatenate([tail[:, :, :, 0:64], tail[:, :, :, 64:128]], axis=1).reshape(1024, 64)
    hid_ref[:, :, 0:128] = find(first_ref[...].reshape(1024, 128)).reshape(64, 8, 128).astype(BF)
    for b in range(5):
        loads[b].wait()
        stores[b].start()
    hid_ref[:, :, 128:192] = find(tail).reshape(64, 8, 64).astype(BF)
    hid_ref[:, :, 192:320] = find(last_ref[...].reshape(1024, 128)).reshape(64, 8, 128).astype(BF)
    for b in range(5):
        stores[b].wait()


def on_device(member_weights, cluster_ids, merge_counts, tokens, routes):
    ys, yr, xr, zr, es, er, bs, br = chunk_shapes()
    hbm = pl.BlockSpec(memory_space=pltpu.HBM)
    vmem = pl.BlockSpec(memory_space=pltpu.VMEM)
    outs = [jax.ShapeDtypeStruct(s, BF) for s in (
        (5, 64, 48, 128), (512, 1024), (8, 8, 16, 128), (8, 4, 16, 128), (8, 8, 16, 128))]
    outs += [jax.ShapeDtypeStruct(s, BF) for s in yr + xr + br]
    scratch = [pltpu.VMEM(s, BF) for s in ys + zr + es + er + bs]
    scratch += [
        pltpu.VMEM((2, 2, 8, 48, 2560), BF),
        pltpu.VMEM((5, 64, 48, 128), BF),
        pltpu.VMEM((64, 768), BF),
        pltpu.VMEM((8, 64, 768), BF),
        pltpu.VMEM((8, 16, 128), BF),
        pltpu.VMEM((8, 8, 16, 768), BF),
        pltpu.VMEM((4, 8, 8, 16, 768), BF),
        pltpu.VMEM((1024, 640), F32),
        pltpu.VMEM((8, 8, 16, W1), BF),
        pltpu.VMEM((8, 8, 16, W2), BF),
        pltpu.VMEM((8, 8, 16, W1), BF),
        pltpu.VMEM((8, 8, 16, W2), BF),
        pltpu.VMEM((8, 4, 16, 128), BF),
        pltpu.VMEM((512, 1024), BF),
        pltpu.VMEM((512, 1024), BF),
        pltpu.VMEM((8, 16, 128), BF),
        pltpu.VMEM((1, 512), jnp.int32),
        pltpu.VMEM((1, 512), F32),
        pltpu.SMEM((1, 512), jnp.int32),
        pltpu.SMEM((1, 512), F32),
        pltpu.SemaphoreType.DMA((NS,)),
        pltpu.SemaphoreType.DMA((NS,)),
        pltpu.SemaphoreType.DMA((NL,)),
    ]
    results = pl.pallas_call(
        kernel,
        out_shape=outs,
        in_specs=[vmem, vmem, vmem, hbm, hbm],
        out_specs=[hbm] * (5 + 3 * NC),
        scratch_shapes=scratch,
        compiler_params=pltpu.CompilerParams(collective_id=0, has_side_effects=True, vmem_limit_bytes=60 * 1024 * 1024),
    )(
        cluster_ids.reshape(1, -1), merge_counts.reshape(1, -1), routes.T, member_weights.reshape(2, 2, 8, 48, 2560), tokens,
    )
    merged, hidden = pl.pallas_call(
        place_results,
        out_shape=[jax.ShapeDtypeStruct((64, 48, 640), BF), jax.ShapeDtypeStruct((64, 8, 320), BF)],
        in_specs=[hbm, vmem, vmem, vmem, vmem],
        out_specs=[hbm, vmem],
        scratch_shapes=[pltpu.VMEM((5, 64, 48, 128), BF), pltpu.SemaphoreType.DMA((5,)), pltpu.SemaphoreType.DMA((5,))],
        compiler_params=pltpu.CompilerParams(vmem_limit_bytes=60 * 1024 * 1024),
    )(*results[:5])
    return merged.reshape(1, 3072, 640), hidden


def solution(mesh):
    return jax.shard_map(
        on_device,
        mesh=mesh,
        in_specs=(P("expert", "tensor", None), P(), P(), P("expert", None), P("expert", None)),
        out_specs=(P("expert", None, "tensor"), P("expert", None, "tensor")),
        check_vma=False,
    )
```

```python
import jax
import jax.numpy as jnp
from jax import lax
from jax.experimental import pallas as pl
from jax.experimental.pallas import tpu as pltpu
from jax.sharding import PartitionSpec as P

MESH = pl.DeviceIdType.MESH
CHUNKS = ((0, 0, 1), (0, 1, 1), (0, 2, 1), (1, 0, 3), (2, 0, 3), (3, 0, 3), (4, 0, 1), (4, 1, 1), (4, 2, 1))
ORDER = (
    "Y1", "TZ", "Y2", "Y7", "U", "X1", "X2", "Y0", "Z1", "Y5", "Y3", "X7", "Z2", "M", "E1", "Y4", "X0", "Z7", "Z0", "B1",
    "X5", "Y8", "E2", "E7", "E0", "Z5", "X3", "Y6", "G1", "X4", "Z3", "E5", "B2", "Z4", "TX", "TY", "T", "E3", "X8",
    "B5", "B0", "G2", "E4", "B3", "X6", "Z8", "G0", "B4", "G5", "S3", "G3", "S0", "Z6", "G4", "E8", "S1", "B7", "E6",
    "B8", "S2", "H", "B6", "G7", "G8", "I", "G6", "S4", "J", "K",
)
NC = len(CHUNKS)
NX, NY, NZ, NP, CAP = 4, 4, 8, 8, 16
W1, W2 = 256, 128
BF = jnp.bfloat16
F32 = jnp.float32


def chunk_shapes():
    ys, yr, xr, zr, es, er, bs, br = [], [], [], [], [], [], [], []
    for _, _, nj in CHUNKS:
        r = 16 * nj
        ys.append((NY, 2, 2, NZ, r, 128))
        yr.append((NY, 2, 2, NZ, r, 128))
        xr.append((NP, 2, NZ, r, 128))
        zr.append((2, 4, NP, 2, r, 128))
        es.append((2, 4, NP, r, 128))
        er.append((2, 4, NP, r, 128))
        bs.append((2, 4, NP, r, 128))
        br.append((NP, NZ, r, 128))
    return ys, yr, xr, zr, es, er, bs, br


S_Y, S_X, S_Z, S_E, S_BZ, S_BX = 0, NC, 2 * NC, 3 * NC, 4 * NC, 5 * NC
S_TZ = 6 * NC
S_SZ, S_TX, S_TY, S_H1X, S_H1Z, S_H1B, S_H2X, S_H2Z = (S_TZ + i for i in range(1, 9))
NS = S_TZ + 9
L_RAW, L_TOK, L_OUT, L_TAB, L_F = 0, 3, 4, 9, 11
NL = 12


def half_tiles(b, t):
    found = []
    for h in range(2):
        col = b * 128 + h * 64
        raw = t * 320 + col if col < 320 else 1280 + t * 320 + col - 320
        found.append((raw // 128, (raw // 64) % 2))
    return found


def kernel(ids_ref, cnt_ref, routes_ref, w_hbm, tok_hbm, *refs):
    out_hbm, f_hbm, hz1, hz1b, hz2 = refs[:5]
    yr, xr, br = (refs[5 + i * NC:5 + (i + 1) * NC] for i in range(3))
    refs = refs[5 + 3 * NC:]
    ys, zr, es, er, bs = (refs[i * NC:(i + 1) * NC] for i in range(5))
    (raw, wv, tsrc, tz, sz, tsel, tok, acc, act1, act2, hx1, hx2, pack, f_ref,
     f_tmp, sel_ref, idx_vmem, wgt_vmem, idx_ref, wgt_ref, ssem, rsem, lsem) = refs[5 * NC:]
    e = lax.axis_index("expert")
    y = lax.axis_index("tensor")
    x, z, k = e // 16, (e // 2) % 8, e % 2
    p = x * 2 + k

    def at_y(t):
        return {"expert": e, "tensor": t}

    def at_z(t):
        return {"expert": x * 16 + t * 2 + k, "tensor": y}

    def at_p(t):
        return {"expert": (t // 2) * 16 + z * 2 + t % 2, "tensor": y}

    groups = ((NY, y, at_y), (NP, p, at_p), (NZ, z, at_z))

    raw_loads = []
    for j in range(3):
        rows = pl.ds(j * 16, 16)
        c = pltpu.make_async_copy(w_hbm.at[:, :, :, rows, :], raw.at[:, :, :, rows, :], lsem.at[L_RAW + j])
        c.start()
        raw_loads.append(c)
        if j == 0:
            tok_load = pltpu.make_async_copy(tok_hbm.at[:, pl.ds(pl.multiple_of(y * 768, 128), 768)], tsrc, lsem.at[L_TOK])
            tok_load.start()
    barrier = pltpu.get_barrier_semaphore()
    for n, me, at in groups:
        def greet(d, carry, n=n, me=me, at=at):
            pl.semaphore_signal(barrier, inc=1, device_id=at((me + d) % n), device_id_type=MESH)
            return carry
        lax.fori_loop(1, n, greet, 0)
    def iota(rows, columns, axis):
        return lax.broadcasted_iota(jnp.int32, (rows, columns), axis)

    drains = []

    def exchange(group, stage, source, target, own=True):
        n, me, at = groups[group]
        if own:
            pltpu.make_async_copy(source(me), target(me), rsem.at[stage]).start()

        def send(d, carry):
            t = (me + d) % n
            pltpu.make_async_remote_copy(
                src_ref=source(t), dst_ref=target(me), send_sem=ssem.at[stage], recv_sem=rsem.at[stage],
                device_id=at(t), device_id_type=MESH,
            ).start()
            return carry

        lax.fori_loop(1, n, send, 0)

    def wait_all(stage, ref):
        pltpu.make_async_copy(ref, ref, rsem.at[stage]).wait()

    def drain(stage, ref):
        drains.append((stage, ref))

    def relayout(c):
        b, j0, nj = CHUNKS[c]
        rows = pl.ds(j0 * 16, nj * 16)
        lane = lax.broadcasted_iota(jnp.int32, (nj * 16, 128), 1)

        def one(i, carry):
            m, kk, zz = i // 16, (i // 8) % 2, i % 8
            for t in range(NY):
                (lo, lo_half), (hi, hi_half) = half_tiles(b, t)
                if lo == hi:
                    ys[c][t, m, kk, zz] = raw[m, kk, zz, rows, lo * 128:lo * 128 + 128]
                    continue
                low = raw[m, kk, zz, rows, lo * 128:lo * 128 + 128].astype(F32)
                high = raw[m, kk, zz, rows, hi * 128:hi * 128 + 128].astype(F32)
                if lo_half == 1:
                    low = pltpu.roll(low, 64, 1)
                if hi_half == 0:
                    high = pltpu.roll(high, 64, 1)
                ys[c][t, m, kk, zz] = jnp.where(lane < 64, low, high).astype(BF)
            return carry

        lax.fori_loop(0, 32, one, 0)

    def stage_y(c):
        exchange(0, S_Y + c, lambda t: ys[c].at[t], lambda s: yr[c].at[s])
        drain(S_Y + c, yr[c].at[pl.ds(0, 3)])

    def stage_x(c):
        wait_all(S_Y + c, yr[c])
        exchange(1, S_X + c, lambda t: yr[c].at[t // 2, :, t % 2], lambda s: xr[c].at[s])
        drain(S_X + c, xr[c].at[pl.ds(0, 7)])

    def send_z(stage, source, target, there):
        pltpu.make_async_remote_copy(
            src_ref=source, dst_ref=target, send_sem=ssem.at[stage], recv_sem=rsem.at[stage],
            device_id=at_z(there), device_id_type=MESH,
        ).start()

    def stage_z(c):
        wait_all(S_X + c, xr[c])
        pltpu.make_async_copy(xr[c].at[:, :, z], zr[c].at[0, 0], rsem.at[S_Z + c]).start()
        pltpu.make_async_copy(xr[c].at[:, :, (z + 7) % 8], zr[c].at[1, 0], rsem.at[S_Z + c]).start()

        def send(i, carry):
            o = 4 - i
            send_z(S_Z + c, xr[c].at[:, :, (z + o) % 8], zr[c].at[0, o], (z + o) % 8)
            send_z(S_Z + c, xr[c].at[:, :, (z + 7 - o) % 8], zr[c].at[1, o], (z + 8 - o) % 8)
            return carry

        lax.fori_loop(1, 4, send, 0)
        drain(S_Z + c, zr[c].at[:, pl.ds(0, 3)])

    def weighted(c, role, entry):
        total = None
        for m in range(4):
            where = idx_ref[0, entry + m]
            term = zr[c][role, (where >> 4) & 3, (where >> 1) & 7, where & 1].astype(F32) * wgt_ref[0, entry + m]
            total = term if total is None else total + term
        return total

    def stage_e(c):
        wait_all(S_Z + c, zr[c])

        def one(i, carry):
            es[c][i // 32, (i // 8) % 4, i % 8] = weighted(c, i // 32, i * 4).astype(BF)
            return carry

        lax.fori_loop(0, 64, one, 0)
        send_z(S_E + c, es[c].at[0], er[c].at[1], (z + 1) % 8)
        send_z(S_E + c, es[c].at[1], er[c].at[0], (z + 7) % 8)
        drain(S_E + c, er[c])

    def stage_bz(c):
        wait_all(S_E + c, er[c])

        def one(i, carry):
            role, plane, owner = i // 32, (i // 8) % 4, i % 8
            total = weighted(c, role, 256 + i * 4) + er[c][role, plane, owner].astype(F32)
            bs[c][role, plane, owner] = total.astype(BF)
            return carry

        lax.fori_loop(0, 64, one, 0)
        low = (z + 7) % 8
        pltpu.make_async_copy(bs[c].at[0, 0], br[c].at[:, z], rsem.at[S_BZ + c]).start()
        pltpu.make_async_copy(bs[c].at[1, 0], br[c].at[:, low], rsem.at[S_BZ + c]).start()

        def send(i, carry):
            o = 4 - i
            send_z(S_BZ + c, bs[c].at[0, o], br[c].at[:, z], (z + 8 - o) % 8)
            send_z(S_BZ + c, bs[c].at[1, o], br[c].at[:, low], (z + o) % 8)
            return carry

        lax.fori_loop(1, 4, send, 0)
        drain(S_BZ + c, br[c].at[pl.ds(0, 6)])

    def stage_bx(c):
        b, j0, nj = CHUNKS[c]
        wait_all(S_BZ + c, br[c])
        exchange(1, S_BX + c, lambda t: br[c].at[t],
                 lambda s: wv.at[b, pl.ds(s * 8, 8), pl.ds(j0 * 16, nj * 16)])
        drain(S_BX + c, wv.at[b, pl.ds(0, 56), pl.ds(j0 * 16, nj * 16)])

    out_copies = []

    ready = []

    def served(b):
        if not ready:
            tokens_done()
            ready.append(True)
        for c, (block, j0, nj) in enumerate(CHUNKS):
            if block == b:
                wait_all(S_BX + c, wv.at[b, :, pl.ds(j0 * 16, nj * 16)])
        copy = pltpu.make_async_copy(wv.at[b], out_hbm.at[b], lsem.at[L_OUT + b])
        copy.start()
        out_copies.append(copy)

        def rows_of(i, carry):
            total = None
            for q in range(NY):
                lhs = tok[q, pl.ds(i * 4, 4)].reshape(512, 768)
                rhs = wv[b, pl.ds(q * 16, 16)].reshape(768, 128)
                part = jnp.dot(lhs, rhs, preferred_element_type=F32)
                total = part if total is None else total + part
            acc[pl.ds(i * 512, 512), b * 128:b * 128 + 128] = total
            return carry

        lax.fori_loop(0, 2, rows_of, 0)

    def silu_up(gate, up):
        return (gate / (1.0 + jnp.exp(-gate))) * up

    def activate_first():
        def one(i, carry):
            r = pl.ds(i * 128, 128)
            hidden = silu_up(acc[r, 0:192], acc[r, 320:512]).astype(BF)
            act1[i] = jnp.concatenate([hidden, jnp.zeros((128, 64), BF)], axis=1).reshape(8, 16, W1)
            return carry

        lax.fori_loop(0, 8, one, 0)

    def activate_second():
        def one(i, carry):
            r = pl.ds(i * 128, 128)
            act2[i] = silu_up(acc[r, 192:320], acc[r, 512:640]).astype(BF).reshape(8, 16, W2)
            return carry

        lax.fori_loop(0, 8, one, 0)

    def hidden_x(stage, act, hx):
        exchange(1, stage, lambda t: act.at[t], lambda s: hx.at[s])
        drain(stage, hx.at[pl.ds(0, 7)])

    def hidden_z_first():
        wait_all(S_H1X, hx1)
        lanes = pl.ds(0, 128)
        exchange(2, S_H1Z, lambda t: hx1.at[:, t, :, lanes], lambda s: hz1.at[s])
        drain(S_H1Z, hz1.at[pl.ds(0, 7)])

        def one(i, carry):
            t, q = i // 4, i % 4
            pack[t, q] = jnp.concatenate([hx1[q, t, :, 128:192], hx1[q + 4, t, :, 128:192]], axis=1)
            return carry

        lax.fori_loop(0, 32, one, 0)
        exchange(2, S_H1B, lambda t: pack.at[t], lambda s: hz1b.at[s])
        drain(S_H1B, hz1b.at[pl.ds(0, 7)])

    def hidden_z_second():
        wait_all(S_H2X, hx2)
        exchange(2, S_H2Z, lambda t: hx2.at[:, t], lambda s: hz2.at[s])
        drain(S_H2Z, hz2.at[pl.ds(0, 7)])

    def tokens_z():
        tok_load.wait()
        exchange(2, S_TZ, lambda t: tsrc, lambda s: tz.at[s])
        select_tokens()
        exchange(2, S_SZ, lambda t: sel_ref.at[t], lambda s: sz.at[s])
        drain(S_SZ, sz.at[pl.ds(0, 7)])
        drain(S_TZ, tz.at[pl.ds(0, 7)])

    def tokens_x():
        wait_all(S_SZ, sz)
        wait_all(S_TZ, tz)
        repeat = jnp.where((iota(128, 16, 0) >> 4) == iota(128, 16, 1), 1.0, 0.0).astype(BF)
        slot = (iota(128, 128, 0) & 15).astype(F32)

        def one(i, carry):
            ranks = jnp.dot(repeat, sz[i], preferred_element_type=F32)
            pick = jnp.where(ranks == slot, 1.0, 0.0)[:, 0:64].astype(BF)
            chosen = jnp.dot(pick, tz[i], preferred_element_type=F32).astype(BF)
            tsel[:, i] = chosen.reshape(8, 16, 768)
            return carry

        lax.fori_loop(0, 8, one, 0)
        exchange(1, S_TX, lambda t: tsel.at[t], lambda s: tok.at[y, s])
        drain(S_TX, tsel.at[pl.ds(0, 7)])

    def tokens_y():
        wait_all(S_TX, tok.at[y])
        exchange(0, S_TY, lambda t: tok.at[y], lambda s: tok.at[s], own=False)
        drain(S_TY, tok.at[pl.ds(0, 3)])

    def tokens_done():
        wait_all(S_TY, tok.at[pl.ds(0, 3)])

    def merge_tables():
        ids, counts = ids_ref[...], cnt_ref[...]
        row, column = iota(128, 128, 0), iota(128, 128, 1)
        ids_down = jnp.sum(jnp.where(row == column, ids, 0), axis=1, keepdims=True)
        counts_down = jnp.sum(jnp.where(row == column, counts, 0), axis=1, keepdims=True)
        same = ids_down == ids
        place = jnp.sum(jnp.where(same & (column < row), 1, 0), axis=1, keepdims=True)
        total = jnp.sum(jnp.where(same, counts, 0), axis=1, keepdims=True)
        weight = counts_down.astype(F32) / total.astype(F32)
        member = iota(128, 512, 0)
        owner = member >> 1
        plane_of = (owner >> 1) & 7
        inside = ((owner >> 4) * 2 + (owner & 1)) * 2 + (member & 1)
        entry = iota(128, 512, 1)
        own, role, i, q, m = entry >> 8, (entry >> 7) & 1, (entry >> 5) & 3, (entry >> 2) & 7, entry & 3
        plane = jnp.where(role == 0, jnp.where(own == 1, z - i, z + 1 + i), jnp.where(own == 1, z + i, z - 1 - i)) & 7
        cluster = (q >> 1) * 16 + plane * 2 + (q & 1)
        away = jnp.where(role == 0, z - plane_of, plane_of - z) & 7
        hit = (ids_down == cluster) & (place == m) & (away < 4)
        idx_vmem[...] = jnp.sum(jnp.where(hit, away * 16 + inside, 0), axis=0, keepdims=True)
        wgt_vmem[...] = jnp.sum(jnp.where(hit, weight, 0.0), axis=0, keepdims=True)
        pltpu.make_async_copy(idx_vmem, idx_ref, lsem.at[L_TAB]).start()
        pltpu.make_async_copy(wgt_vmem, wgt_ref, lsem.at[L_TAB + 1]).start()

    def merge_tables_done():
        pltpu.make_async_copy(idx_vmem, idx_ref, lsem.at[L_TAB]).wait()
        pltpu.make_async_copy(wgt_vmem, wgt_ref, lsem.at[L_TAB + 1]).wait()

    def slot_ranks():
        unit = jnp.where(iota(64, 64, 0) == iota(64, 64, 1), 1.0, 0.0).astype(BF)
        turned = routes_ref[...].astype(F32).astype(BF)
        routes = lax.dot_general(unit, turned, (((1,), (1,)), ((), ())), preferred_element_type=F32).astype(jnp.int32)
        hits = [jnp.where(routes[:, j:j + 1] == iota(64, 64, 1), 1.0, 0.0) for j in range(8)]
        named = sum(hits[1:], hits[0])
        lower = jnp.where(iota(64, 64, 1) < iota(64, 64, 0), 1.0, 0.0).astype(BF)
        rank = jnp.dot(lower, named.astype(BF), preferred_element_type=F32)
        return routes, hits, named, rank

    def select_tokens():
        routes, hits, named, rank = slot_ranks()
        tagged = jnp.where(named > 0.0, rank, -1.0)
        tagged = jnp.concatenate([tagged, jnp.full((64, 64), -1.0, F32)], axis=0).astype(BF)
        unit = jnp.where(iota(64, 64, 0) == iota(64, 64, 1), 1.0, 0.0).astype(BF)
        across = lax.dot_general(unit, tagged, (((1,), (1,)), ((), ())), preferred_element_type=F32).astype(BF)
        row = iota(128, 64, 0)
        cluster = ((row & 15) >> 1) * 16 + (row >> 4) * 2 + (row & 1)
        spread = jnp.where(cluster == iota(128, 64, 1), 1.0, 0.0).astype(BF)
        sel_ref[...] = jnp.dot(spread, across, preferred_element_type=F32).astype(BF).reshape(8, 16, 128)

    def find_slots():
        routes, hits, named, rank = slot_ranks()
        for j in range(8):
            mine = jnp.sum(hits[j] * rank, axis=1, keepdims=True).astype(jnp.int32)
            r = routes[:, j:j + 1]
            slot = ((r >> 1) & 7) * 128 + ((r >> 4) * 2 + (r & 1)) * CAP + mine
            f_tmp[j * 64:j * 64 + 64, :] = jnp.where(slot == iota(64, 1024, 1), 1.0, 0.0).astype(BF)

        def one(i, carry):
            row = iota(128, 512, 0) + i * 128
            order = jnp.where(iota(128, 512, 1) == (row & 7) * 64 + (row >> 3), 1.0, 0.0).astype(BF)
            f_ref[pl.ds(i * 128, 128), :] = jnp.dot(order, f_tmp[...], preferred_element_type=F32).astype(BF)
            return carry

        lax.fori_loop(0, 4, one, 0)
        copy = pltpu.make_async_copy(f_ref, f_hbm, lsem.at[L_F])
        copy.start()
        out_copies.append(copy)

    loaded = set()
    early = set()

    def first(c):
        b, j0, nj = CHUNKS[c]
        for j in range(j0, j0 + nj):
            if j not in loaded:
                loaded.add(j)
                raw_loads[j].wait()
        if c not in early:
            relayout(c)
        stage_y(c)

    def third():
        activate_first()
        hidden_x(S_H1X, act1, hx1)

    def fourth():
        activate_second()
        hidden_x(S_H2X, act2, hx2)

    stages = {"Y": first, "X": stage_x, "Z": stage_z, "E": stage_e, "B": stage_bz, "G": stage_bx, "S": served}
    once = {
        "U": merge_tables, "M": merge_tables_done, "T": find_slots, "TZ": tokens_z, "TX": tokens_x, "TY": tokens_y, "H": third, "J": fourth,
        "I": hidden_z_first, "K": hidden_z_second,
    }
    opening = int(next(step for step in ORDER if step[0] == "Y")[1:])
    for j in range(CHUNKS[opening][1], CHUNKS[opening][1] + CHUNKS[opening][2]):
        raw_loads[j].wait()
        loaded.add(j)
    relayout(opening)
    early.add(opening)
    pl.semaphore_wait(barrier, NY + NP + NZ - 3)
    for step in ORDER:
        if step in once:
            once[step]()
        else:
            stages[step[0]](int(step[1:]))

    wait_all(S_H1Z, hz1)
    wait_all(S_H1B, hz1b)
    wait_all(S_H2Z, hz2)
    for copy in out_copies:
        copy.wait()
    for stage, ref in drains:
        pltpu.make_async_copy(ref, ref, ssem.at[stage]).wait()


def place_results(blocks, f_ref, first_ref, tail_ref, last_ref, out_hbm, hid_ref, held, load_sem, store_sem):
    loads, stores = [], []
    for b in range(5):
        loads.append(pltpu.make_async_copy(blocks.at[b], held.at[b], load_sem.at[b]))
        stores.append(pltpu.make_async_copy(held.at[b], out_hbm.at[:, :, pl.ds(b * 128, 128)], store_sem.at[b]))
        loads[b].start()

    def find(rows):
        return jnp.dot(f_ref[...], rows, preferred_element_type=F32)

    for b in range(5):
        loads[b].wait()
        stores[b].start()
    tail = tail_ref[...]
    tail = jnp.concatenate([tail[:, :, :, 0:64], tail[:, :, :, 64:128]], axis=1).reshape(1024, 64)
    hid_ref[:, :, 0:128] = find(first_ref[...].reshape(1024, 128)).reshape(64, 8, 128).astype(BF)
    hid_ref[:, :, 128:192] = find(tail).reshape(64, 8, 64).astype(BF)
    hid_ref[:, :, 192:320] = find(last_ref[...].reshape(1024, 128)).reshape(64, 8, 128).astype(BF)
    for b in range(5):
        stores[b].wait()


def on_device(member_weights, cluster_ids, merge_counts, tokens, routes):
    ys, yr, xr, zr, es, er, bs, br = chunk_shapes()
    hbm = pl.BlockSpec(memory_space=pltpu.HBM)
    vmem = pl.BlockSpec(memory_space=pltpu.VMEM)
    outs = [jax.ShapeDtypeStruct(s, BF) for s in (
        (5, 64, 48, 128), (512, 1024), (8, 8, 16, 128), (8, 4, 16, 128), (8, 8, 16, 128))]
    outs += [jax.ShapeDtypeStruct(s, BF) for s in yr + xr + br]
    scratch = [pltpu.VMEM(s, BF) for s in ys + zr + es + er + bs]
    scratch += [
        pltpu.VMEM((2, 2, 8, 48, 2560), BF),
        pltpu.VMEM((5, 64, 48, 128), BF),
        pltpu.VMEM((64, 768), BF),
        pltpu.VMEM((8, 64, 768), BF),
        pltpu.VMEM((8, 16, 128), BF),
        pltpu.VMEM((8, 8, 16, 768), BF),
        pltpu.VMEM((4, 8, 8, 16, 768), BF),
        pltpu.VMEM((1024, 640), F32),
        pltpu.VMEM((8, 8, 16, W1), BF),
        pltpu.VMEM((8, 8, 16, W2), BF),
        pltpu.VMEM((8, 8, 16, W1), BF),
        pltpu.VMEM((8, 8, 16, W2), BF),
        pltpu.VMEM((8, 4, 16, 128), BF),
        pltpu.VMEM((512, 1024), BF),
        pltpu.VMEM((512, 1024), BF),
        pltpu.VMEM((8, 16, 128), BF),
        pltpu.VMEM((1, 512), jnp.int32),
        pltpu.VMEM((1, 512), F32),
        pltpu.SMEM((1, 512), jnp.int32),
        pltpu.SMEM((1, 512), F32),
        pltpu.SemaphoreType.DMA((NS,)),
        pltpu.SemaphoreType.DMA((NS,)),
        pltpu.SemaphoreType.DMA((NL,)),
    ]
    results = pl.pallas_call(
        kernel,
        out_shape=outs,
        in_specs=[vmem, vmem, vmem, hbm, hbm],
        out_specs=[hbm] * (5 + 3 * NC),
        scratch_shapes=scratch,
        compiler_params=pltpu.CompilerParams(collective_id=0, has_side_effects=True, vmem_limit_bytes=60 * 1024 * 1024),
    )(
        cluster_ids.reshape(1, -1), merge_counts.reshape(1, -1), routes.T, member_weights.reshape(2, 2, 8, 48, 2560), tokens,
    )
    merged, hidden = pl.pallas_call(
        place_results,
        out_shape=[jax.ShapeDtypeStruct((64, 48, 640), BF), jax.ShapeDtypeStruct((64, 8, 320), BF)],
        in_specs=[hbm, vmem, vmem, vmem, vmem],
        out_specs=[hbm, vmem],
        scratch_shapes=[pltpu.VMEM((5, 64, 48, 128), BF), pltpu.SemaphoreType.DMA((5,)), pltpu.SemaphoreType.DMA((5,))],
        compiler_params=pltpu.CompilerParams(vmem_limit_bytes=60 * 1024 * 1024),
    )(*results[:5])
    return merged.reshape(1, 3072, 640), hidden


def solution(mesh):
    return jax.shard_map(
        on_device,
        mesh=mesh,
        in_specs=(P("expert", "tensor", None), P(), P(), P("expert", None), P("expert", None)),
        out_specs=(P("expert", None, "tensor"), P("expert", None, "tensor")),
        check_vma=False,
    )
```
